256 devices in a mesh: lat: 64 (over y, x, z_lo), rad: 4 (over z_hi, core).
Axes of the slice: x: 4, y: 4, z: 8 (z_hi: 2, z_lo: 4; z = z_hi * 4 + z_lo), core: 2. Of those that a mesh axis runs over, the one named last changes fastest.
Arguments:
- source: float32 [16, 1024, 1024], P('rad', 'lat'), may hold values from -8 to 8
- kappa: float32 [16, 1024, 1024], P('rad', 'lat'), may hold values from 0.02 to 0.5
- forward: float32 [16, 1024, 1024], P('rad', 'lat'), may hold values from -8 to 8
- viscosity: float32 [16, 1024, 1024], P('rad', 'lat'), may hold values from 0.1 to 10
Outputs:
- adjoint: float32 [16, 1024, 1024], P('rad', 'lat')
- gradient: float32 [16, 1024, 1024], P('rad', 'lat')
The draws below stay inside these ranges and needn't reach their ends.
All inputs are finite; a program needn't handle non-finite values.
Results may differ from the reference program's by a relative error of at most 0.00002.
Values sent between devices are 32-bit elements; how exact they have to be, the bound alone decides.
No kernel may reach another device: no remote copies, remote signals or barrier semaphores. Data moves between devices by JAX's collectives and lax.ppermute only.
A program may use at most 128 MiB of HBM per device.

```python
import math
import jax
import jax.numpy as jnp

NY = 1024
S_F = 8
S_C = 8
NR = 16
NX = 1024


def shard_levels(key, shape, cuts, smallest, largest):
    loudness = 1.0
    for position, parts in cuts:
        heights = jax.random.uniform(jax.random.fold_in(jax.random.fold_in(key, 6), position), (parts,), jnp.float32, smallest / len(cuts), largest / len(cuts))
        loudness = loudness * jnp.repeat(jnp.exp(heights), shape[position] // parts).reshape((-1,) + (1,) * (len(shape) - 1 - position))
    return loudness


def scatter_about(rng, shape, deviation, reach, split=(), dtype=jnp.bfloat16):
    entries = deviation * jax.random.normal(rng, shape, jnp.float32)
    if split:
        entries = entries * shard_levels(rng, shape, split, -0.22, 0.18)
    return jnp.clip(entries, -reach, reach).astype(dtype)


def setup_inputs(seed: int = 0) -> dict:
    seeds = jax.random.split(jax.random.key(seed), 5)
    source = scatter_about(seeds[0], (NR, NX, NY), 1.0, 8.0, ((0, 4), (1, 64)), jnp.float32)
    kappa = jnp.clip(jnp.exp(math.log(0.5) - 3.218876 * jax.random.uniform(seeds[1], (NR, NX, NY), jnp.float32) ** shard_levels(seeds[1], (NR, NX, NY), ((0, 4), (1, 64)), -0.2, 0.2)), 0.02, 0.5)
    forward = scatter_about(seeds[2], (NR, NX, NY), 1.0, 8.0, ((0, 4), (1, 64)), jnp.float32)
    viscosity = jnp.clip(jnp.exp(math.log(10.0) - 4.6051702 * jax.random.uniform(seeds[3], (NR, NX, NY), jnp.float32) ** shard_levels(seeds[3], (NR, NX, NY), ((0, 4), (1, 64)), -0.2, 0.2)), 0.1, 10.0)
    return {"source": source, "kappa": kappa, "forward": forward, "viscosity": viscosity}


def neighbours(v):
    zero = jnp.zeros_like(v[:1])
    up = jnp.concatenate([v[1:], zero], axis=0)
    down = jnp.concatenate([zero, v[:-1]], axis=0)
    lateral = jnp.roll(v, 1, 1) + jnp.roll(v, -1, 1) + jnp.roll(v, 1, 2) + jnp.roll(v, -1, 2)
    return lateral + up + down


def chebyshev(rhs, apply_op, low, high, sweeps):
    theta = (high + low) / 2.0
    delta = (high - low) / 2.0
    sigma = theta / delta
    rho = 1.0 / sigma
    solved = jnp.zeros_like(rhs)
    resid = rhs
    direction = rhs / theta
    for sweep in range(sweeps):
        solved = solved + direction
        resid = resid - apply_op(direction)
        rho_new = 1.0 / (2.0 * sigma - rho)
        direction = rho_new * rho * direction + (2.0 * rho_new / delta) * resid
        rho = rho_new
    return solved, resid


def coarsen(v):
    a, b, c = v.shape
    return v.reshape(a // 2, 2, b // 2, 2, c // 2, 2).mean(axis=(1, 3, 5))


def refine(v):
    return jnp.repeat(jnp.repeat(jnp.repeat(v, 2, 0), 2, 1), 2, 2)


def forward_diffs(v):
    zero = jnp.zeros_like(v[:1])
    up = jnp.concatenate([v[1:], zero], axis=0)
    return (up - v, jnp.roll(v, -1, 1) - v, jnp.roll(v, -1, 2) - v)


def reference(source, kappa, forward, viscosity):
    def fine_op(v):
        return (6.0 + kappa) * v - neighbours(v)
    smooth, fine_residual = chebyshev(source, fine_op, 1.5, 12.5, S_F)
    coarse_rhs = coarsen(fine_residual)
    coarse_kappa = coarsen(kappa)

    def coarse_op(v):
        return 0.25 * ((6.0 + 4.0 * coarse_kappa) * v - neighbours(v))
    correction, unused = chebyshev(coarse_rhs, coarse_op, 0.05, 3.5, S_C)
    adjoint = smooth + refine(correction)
    first = forward_diffs(forward)
    second = forward_diffs(adjoint)
    gradient = viscosity * (first[0] * second[0] + first[1] * second[1] + first[2] * second[2])
    return adjoint, gradient
```

```python
import jax
import jax.numpy as jnp
from jax import lax
from jax.experimental import pallas as pl
from jax.experimental.pallas import tpu as pltpu
from jax.sharding import PartitionSpec as P

S_F = 8
S_C = 8
FINE = (1.5, 12.5)
COARSE = (0.05, 3.5)

LAYERS = 4
ROWS = 16
NR = 16
HALO = 8
MAIN = 256
WIDE = 384
PACKED = 640
EDGE = 32
VMEM = pltpu.CompilerParams(vmem_limit_bytes=40 * 1024 * 1024)
F32 = jnp.float32


def lanes(shape):
    return lax.broadcasted_iota(jnp.int32, shape, len(shape) - 1)


def coefficients(low, high, sweeps):
    theta = (high + low) / 2.0
    delta = (high - low) / 2.0
    sigma = theta / delta
    rho = 1.0 / sigma
    pairs = []
    for _ in range(sweeps):
        rho_new = 1.0 / (2.0 * sigma - rho)
        pairs.append((rho_new * rho, 2.0 * rho_new / delta))
        rho = rho_new
    return 1.0 / theta, pairs


def pack_windows(ids, source, kappa, *outs):
    lane = lanes((LAYERS, ROWS, 128))
    right = lane < EDGE
    left = lane >= 128 - EDGE
    for m, out in enumerate(outs):
        base = ids[m] * MAIN
        main = pl.ds(pl.multiple_of(base, 128), MAIN)
        after = pl.ds(pl.multiple_of(lax.rem(base + MAIN, 1024), 128), 128)
        before = pl.ds(pl.multiple_of(lax.rem(base + 1024 - 128, 1024), 128), 128)
        out[:, :, 0:MAIN] = source[:, :, main]
        out[:, :, MAIN : 2 * MAIN] = kappa[:, :, main]
        edge_s = jnp.where(right, source[:, :, after], source[:, :, before])
        edge_k = jnp.where(right, kappa[:, :, after], kappa[:, :, before])
        edge_k = pltpu.roll(edge_k, 64, 2)
        out[:, :, 2 * MAIN :] = jnp.where(right | left, edge_s, edge_k)


def pack_rows(ids, p0, p1, p2, p3, up, down):
    for m, piece in enumerate((p0, p1, p2, p3)):
        at = pl.ds((ids[4] ^ m) * LAYERS, LAYERS)
        up[at] = piece[:, HALO:, :]
        down[at] = piece[:, :HALO, :]


def spread(packed, rhs, diag):
    lane = lanes(packed.shape[:-1] + (128,))
    keep = (lane < EDGE) | (lane >= 128 - EDGE)
    edge = packed[..., 2 * MAIN :]
    rhs_edge = jnp.where(keep, edge, 0.0)
    diag_edge = jnp.where(keep, pltpu.roll(edge, 64, edge.ndim - 1), 0.0)
    rhs[..., :MAIN] = packed[..., :MAIN]
    rhs[..., MAIN:] = rhs_edge
    diag[..., :MAIN] = packed[..., MAIN : 2 * MAIN] + 6.0
    diag[..., MAIN:] = diag_edge + 6.0


def lateral(v, step_x, step_y):
    rows, width = v.shape
    return (
        pltpu.roll(v, step_x, 0)
        + pltpu.roll(v, rows - step_x, 0)
        + pltpu.roll(v, step_y, 1)
        + pltpu.roll(v, width - step_y, 1)
    )


def fine_kernel(ids, p0, p1, p2, p3, lo, hi, smooth, packed, rhs, diag, xa, xb, step):
    me = ids[4]
    for m, piece in enumerate((p0, p1, p2, p3)):
        base = (me ^ m) * LAYERS

        def fill(j, _, piece=piece, base=base):
            own = pl.ds(HALO, ROWS)
            spread(piece[j], rhs.at[base + j, own], diag.at[base + j, own])
            return 0

        lax.fori_loop(0, LAYERS, fill, 0)

    first, pairs = coefficients(*FINE, S_F)
    zero = jnp.zeros((2 * ROWS, WIDE), F32)
    xa[0] = zero
    xb[0] = zero
    xa[NR + 1] = zero
    xb[NR + 1] = zero

    def begin(r, _):
        spread(lo[r], rhs.at[r, pl.ds(0, HALO)], diag.at[r, pl.ds(0, HALO)])
        top = pl.ds(HALO + ROWS, HALO)
        spread(hi[r], rhs.at[r, top], diag.at[r, top])
        d = rhs[r] * first
        step[r] = d
        xa[r + 1] = d
        return 0

    lax.fori_loop(0, NR, begin, 0)

    old, new = xa, xb
    for damp, gain in pairs[: S_F - 1]:

        def sweep(r, _, old=old, new=new, damp=damp, gain=gain):
            v = old[r + 1]
            near = old[r] + old[r + 2] + lateral(v, 1, 1)
            resid = rhs[r] - diag[r] * v + near
            d = damp * step[r] + gain * resid
            step[r] = d
            new[r + 1] = v + d
            return 0

        lax.fori_loop(0, NR, sweep, 0)
        old, new = new, old

    even_row = lax.rem(lax.broadcasted_iota(jnp.int32, (ROWS, WIDE), 0), 2) == 0
    even_lane = lax.rem(lanes((HALO, WIDE)), 2) == 0
    pick_r = lax.broadcasted_iota(jnp.int32, (HALO, ROWS), 0)
    pick_c = lax.broadcasted_iota(jnp.int32, (HALO, ROWS), 1)
    pick = jnp.where(lax.shift_right_logical(pick_c, 1) == pick_r, 0.125, 0.0).astype(F32)

    def block_mean(v):
        s = jnp.dot(pick, v, precision=lax.Precision.HIGHEST, preferred_element_type=F32)
        return s + jnp.where(even_lane, pltpu.roll(s, WIDE - 1, 1), pltpu.roll(s, 1, 1))

    def residual(q, _):
        total = None
        diags = None
        for j in range(2):
            r = 2 * q + j
            v = old[r + 1]
            near = old[r] + old[r + 2] + lateral(v, 1, 1)
            resid = (rhs[r] - diag[r] * v + near)[HALO : HALO + ROWS]
            total = resid if total is None else total + resid
            k = diag[r, HALO : HALO + ROWS] - 6.0
            diags = k if diags is None else diags + k
            smooth[r] = v[HALO:, :MAIN]
        packed[q] = jnp.where(even_lane, block_mean(total), block_mean(diags))
        return 0

    lax.fori_loop(0, NR // 2, residual, 0)


def coarse_kernel(ids, lo, own, hi, smooth, o0, o1, o2, o3, rhs, diag, xa, xb, step, adj):
    first, pairs = coefficients(*COARSE, S_C)
    half = NR // 2
    rows = 3 * HALO
    zero = jnp.zeros((rows, WIDE), F32)
    xa[0] = zero
    xb[0] = zero
    xa[half + 1] = zero
    xb[half + 1] = zero
    even = lax.rem(lanes((HALO, WIDE)), 2) == 0

    def begin(q, _):
        for part, src in enumerate((lo, own, hi)):
            v = src[q]
            at = pl.ds(part * HALO, HALO)
            rhs[q, at] = jnp.where(even, v, pltpu.roll(v, 1, 1))
            diag[q, at] = jnp.where(even, pltpu.roll(v, WIDE - 1, 1), v) + 1.5
        d = rhs[q] * first
        step[q] = d
        xa[q + 1] = d
        return 0

    lax.fori_loop(0, half, begin, 0)
    old, new = xa, xb
    for damp, gain in pairs[: S_C - 1]:

        def sweep(q, _, old=old, new=new, damp=damp, gain=gain):
            v = old[q + 1]
            near = old[q] + old[q + 2] + lateral(v, 1, 2)
            resid = rhs[q] - diag[q] * v + 0.25 * near
            d = damp * step[q] + gain * resid
            step[q] = d
            new[q + 1] = v + d
            return 0

        lax.fori_loop(0, half, sweep, 0)
        old, new = new, old

    copy_r = lax.broadcasted_iota(jnp.int32, (rows, 2 * HALO), 0)
    copy_c = lax.broadcasted_iota(jnp.int32, (rows, 2 * HALO), 1)
    copy = jnp.where(lax.shift_right_logical(copy_r, 1) == copy_c, 1.0, 0.0).astype(F32)

    def refine(q, _):
        c = jnp.dot(copy, old[q + 1, HALO:, :MAIN], precision=lax.Precision.HIGHEST, preferred_element_type=F32)
        for j in range(2):
            adj[2 * q + j] = smooth[2 * q + j] + c
        return 0

    lax.fori_loop(0, half, refine, 0)
    adj[NR] = jnp.zeros((rows, MAIN), F32)
    for m, out in enumerate((o0, o1, o2, o3)):
        base = (ids[4] ^ m) * LAYERS
        for j in range(LAYERS + 1):
            out[2 * j] = adj[base + j, 0:8]
            out[2 * j + 1] = adj[base + j, 8:16]
        for j in range(LAYERS):
            out[2 * LAYERS + 2, pl.ds(j, 1)] = adj[base + j, 16:17]
        out[2 * LAYERS + 2, pl.ds(LAYERS, 4)] = jnp.zeros((4, MAIN), F32)


def gradient_kernel(ids, p0, p1, p2, p3, forward, forward_x, forward_r, viscosity, adjoint, gradient, above, beyond):
    for m, piece in enumerate((p0, p1, p2, p3)):
        at = pl.ds(pl.multiple_of(ids[m] * MAIN, 128), MAIN)
        for j in range(LAYERS):
            adjoint[j, 0:8, at] = piece[2 * j]
            adjoint[j, 8:16, at] = piece[2 * j + 1]
        above[0:8, at] = piece[2 * LAYERS]
        above[8:16, at] = piece[2 * LAYERS + 1]
        beyond[:, at] = piece[2 * LAYERS + 2]
    last = lax.broadcasted_iota(jnp.int32, (ROWS, 1024), 0) == ROWS - 1
    for j in range(LAYERS):
        a = adjoint[j]
        f = forward[j]
        a_r = (adjoint[j + 1] if j + 1 < LAYERS else above[...]) - a
        f_r = (forward[j + 1] if j + 1 < LAYERS else forward_r[0]) - f
        a_x = jnp.where(last, beyond[pl.ds(j, 1)], pltpu.roll(a, ROWS - 1, 0)) - a
        f_x = jnp.where(last, forward_x[j], pltpu.roll(f, ROWS - 1, 0)) - f
        a_y = pltpu.roll(a, 1023, 1) - a
        f_y = pltpu.roll(f, 1023, 1) - f
        gradient[j] = viscosity[j] * (f_r * a_r + f_x * a_x + f_y * a_y)


def struct(*shape):
    return jax.ShapeDtypeStruct(shape, F32)


def call(kernel, outs, scratch, ids, *args):
    whole = pl.BlockSpec(memory_space=pltpu.VMEM)
    return pl.pallas_call(
        kernel,
        out_shape=outs,
        in_specs=[pl.BlockSpec(memory_space=pltpu.SMEM)] + [whole] * len(args),
        out_specs=[whole] * len(outs),
        scratch_shapes=[pltpu.VMEM(s, F32) for s in scratch],
        compiler_params=VMEM,
    )(ids, *args)


def body(source, kappa, forward, viscosity):
    lat_n = lax.axis_size("lat")
    rad_n = lax.axis_size("rad")
    lat = lax.axis_index("lat")
    rad = lax.axis_index("rad")

    def flip(i):
        return ((i // 4) % 2) * 2

    turn = flip(lat)
    ids = jnp.stack([rad ^ turn, rad ^ 1 ^ turn, rad ^ 2 ^ turn, rad ^ 3 ^ turn, rad]).astype(jnp.int32)

    def trade(pieces):
        out = [pieces[0]]
        for m in range(1, rad_n):
            out.append(lax.ppermute(pieces[m], "rad", [(k, k ^ m) for k in range(rad_n)]))
        return out

    def beside(v, way):
        pairs = []
        for i in range(lat_n):
            to = (i + way) % lat_n
            for k in range(rad_n):
                pairs.append((i * rad_n + k, to * rad_n + (k ^ flip(i) ^ flip(to))))
        return lax.ppermute(v, ("lat", "rad"), pairs)

    pieces = call(pack_windows, [struct(LAYERS, ROWS, PACKED)] * 4, [], ids, source, kappa)
    pieces = trade(pieces)
    up, down = call(pack_rows, [struct(NR, HALO, PACKED)] * 2, [], ids, *pieces)
    lo = beside(up, 1)
    hi = beside(down, -1)
    deep = (NR, 2 * ROWS, WIDE)
    padded = (NR + 2, 2 * ROWS, WIDE)
    smooth, packed = call(
        fine_kernel,
        [struct(NR, 3 * HALO, MAIN), struct(NR // 2, HALO, WIDE)],
        [deep, deep, padded, padded, deep],
        ids,
        *pieces,
        lo,
        hi,
    )
    below = beside(packed, 1)
    over = beside(packed, -1)
    deep = (NR // 2, 3 * HALO, WIDE)
    padded = (NR // 2 + 2, 3 * HALO, WIDE)
    backs = call(
        coarse_kernel,
        [struct(2 * LAYERS + 3, 8, MAIN)] * 4,
        [deep, deep, padded, padded, deep, (NR + 1, 3 * HALO, MAIN)],
        ids,
        below,
        packed,
        over,
        smooth,
    )
    backs = trade(backs)
    forward_x = lax.ppermute(forward[:, :1], "lat", [((i + 1) % lat_n, i) for i in range(lat_n)])
    forward_r = lax.ppermute(forward[:1], "rad", [(k + 1, k) for k in range(rad_n - 1)])
    adjoint, gradient = call(
        gradient_kernel,
        [struct(LAYERS, ROWS, 1024)] * 2,
        [(ROWS, 1024), (8, 1024)],
        ids,
        *backs,
        forward,
        forward_x,
        forward_r,
        viscosity,
    )
    return adjoint, gradient


def solution(mesh):
    placed = P("rad", "lat", None)
    return jax.shard_map(
        body,
        mesh=mesh,
        in_specs=(placed,) * 4,
        out_specs=(placed,) * 2,
        check_vma=False,
    )
```

```python
import jax
import jax.numpy as jnp
from jax import lax
from jax.experimental import pallas as pl
from jax.experimental.pallas import tpu as pltpu
from jax.sharding import PartitionSpec as P

S_F = 8
S_C = 8
FINE = (1.5, 12.5)
COARSE = (0.05, 3.5)

LAYERS = 4
ROWS = 16
NR = 16
HALO = 8
MAIN = 256
WIDE = 384
PACKED = 640
EDGE = 32
VMEM = pltpu.CompilerParams(vmem_limit_bytes=40 * 1024 * 1024)
F32 = jnp.float32


def lanes(shape):
    return lax.broadcasted_iota(jnp.int32, shape, len(shape) - 1)


def coefficients(low, high, sweeps):
    theta = (high + low) / 2.0
    delta = (high - low) / 2.0
    sigma = theta / delta
    rho = 1.0 / sigma
    pairs = []
    for _ in range(sweeps):
        rho_new = 1.0 / (2.0 * sigma - rho)
        pairs.append((rho_new * rho, 2.0 * rho_new / delta))
        rho = rho_new
    return 1.0 / theta, pairs


def pack_windows(ids, source_hbm, kappa_hbm, *refs):
    outs, (source, kappa, done) = refs[:4], refs[4:]
    loads = []
    for f, (src, dst) in enumerate(((source_hbm, source), (kappa_hbm, kappa))):
        for j in range(LAYERS):
            loads.append(pltpu.make_async_copy(src.at[j], dst.at[j], done.at[f, j]))
            loads[-1].start()
    for load in loads:
        load.wait()
    lane = lanes((LAYERS, ROWS, 128))
    right = lane < EDGE
    left = lane >= 128 - EDGE
    for m, out in enumerate(outs):
        base = ids[m] * MAIN
        main = pl.ds(pl.multiple_of(base, 128), MAIN)
        after = pl.ds(pl.multiple_of(lax.rem(base + MAIN, 1024), 128), 128)
        before = pl.ds(pl.multiple_of(lax.rem(base + 1024 - 128, 1024), 128), 128)
        out[:, :, 0:MAIN] = source[:, :, main]
        out[:, :, MAIN : 2 * MAIN] = kappa[:, :, main]
        edge_s = jnp.where(right, source[:, :, after], source[:, :, before])
        edge_k = jnp.where(right, kappa[:, :, after], kappa[:, :, before])
        edge_k = pltpu.roll(edge_k, 64, 2)
        out[:, :, 2 * MAIN :] = jnp.where(right | left, edge_s, edge_k)


def pack_rows(ids, p0, p1, p2, p3, up, down):
    for m, piece in enumerate((p0, p1, p2, p3)):
        at = pl.ds((ids[4] ^ m) * LAYERS, LAYERS)
        up[at] = piece[:, HALO:, :]
        down[at] = piece[:, :HALO, :]


def spread(packed, rhs, diag):
    lane = lanes(packed.shape[:-1] + (128,))
    keep = (lane < EDGE) | (lane >= 128 - EDGE)
    edge = packed[..., 2 * MAIN :]
    rhs_edge = jnp.where(keep, edge, 0.0)
    diag_edge = jnp.where(keep, pltpu.roll(edge, 64, edge.ndim - 1), 0.0)
    rhs[..., :MAIN] = packed[..., :MAIN]
    rhs[..., MAIN:] = rhs_edge
    diag[..., :MAIN] = packed[..., MAIN : 2 * MAIN] + 6.0
    diag[..., MAIN:] = diag_edge + 6.0


def lateral(v, step_x, step_y):
    rows, width = v.shape
    return (
        pltpu.roll(v, step_x, 0)
        + pltpu.roll(v, rows - step_x, 0)
        + pltpu.roll(v, step_y, 1)
        + pltpu.roll(v, width - step_y, 1)
    )


def fine_kernel(ids, p0, p1, p2, p3, lo, hi, smooth, packed, rhs, diag, xa, xb, step):
    me = ids[4]
    for m, piece in enumerate((p0, p1, p2, p3)):
        base = (me ^ m) * LAYERS

        def fill(j, _, piece=piece, base=base):
            own = pl.ds(HALO, ROWS)
            spread(piece[j], rhs.at[base + j, own], diag.at[base + j, own])
            return 0

        lax.fori_loop(0, LAYERS, fill, 0, unroll=True)

    first, pairs = coefficients(*FINE, S_F)
    zero = jnp.zeros((2 * ROWS, WIDE), F32)
    xa[0] = zero
    xb[0] = zero
    xa[NR + 1] = zero
    xb[NR + 1] = zero

    def begin(r, _):
        spread(lo[r], rhs.at[r, pl.ds(0, HALO)], diag.at[r, pl.ds(0, HALO)])
        top = pl.ds(HALO + ROWS, HALO)
        spread(hi[r], rhs.at[r, top], diag.at[r, top])
        d = rhs[r] * first
        step[r] = d
        xa[r + 1] = d
        return 0

    lax.fori_loop(0, NR, begin, 0, unroll=True)

    old, new = xa, xb
    for damp, gain in pairs[: S_F - 1]:

        def sweep(r, _, old=old, new=new, damp=damp, gain=gain):
            v = old[r + 1]
            near = old[r] + old[r + 2] + lateral(v, 1, 1)
            resid = rhs[r] - diag[r] * v + near
            d = damp * step[r] + gain * resid
            step[r] = d
            new[r + 1] = v + d
            return 0

        lax.fori_loop(0, NR, sweep, 0, unroll=True)
        old, new = new, old

    even_row = lax.rem(lax.broadcasted_iota(jnp.int32, (ROWS, WIDE), 0), 2) == 0
    even_lane = lax.rem(lanes((HALO, WIDE)), 2) == 0
    pick_r = lax.broadcasted_iota(jnp.int32, (HALO, ROWS), 0)
    pick_c = lax.broadcasted_iota(jnp.int32, (HALO, ROWS), 1)
    pick = jnp.where(lax.shift_right_logical(pick_c, 1) == pick_r, 0.125, 0.0).astype(F32)

    def block_mean(v):
        s = jnp.dot(pick, v, precision=lax.Precision.HIGHEST, preferred_element_type=F32)
        return s + jnp.where(even_lane, pltpu.roll(s, WIDE - 1, 1), pltpu.roll(s, 1, 1))

    def residual(q, _):
        total = None
        diags = None
        for j in range(2):
            r = 2 * q + j
            v = old[r + 1]
            near = old[r] + old[r + 2] + lateral(v, 1, 1)
            resid = (rhs[r] - diag[r] * v + near)[HALO : HALO + ROWS]
            total = resid if total is None else total + resid
            k = diag[r, HALO : HALO + ROWS] - 6.0
            diags = k if diags is None else diags + k
            smooth[r] = v[HALO:, :MAIN]
        packed[q] = jnp.where(even_lane, block_mean(total), block_mean(diags))
        return 0

    lax.fori_loop(0, NR // 2, residual, 0, unroll=True)


def coarse_kernel(ids, lo, own, hi, smooth, o0, o1, o2, o3, rhs, diag, xa, xb, step, adj):
    first, pairs = coefficients(*COARSE, S_C)
    half = NR // 2
    rows = 3 * HALO
    zero = jnp.zeros((rows, WIDE), F32)
    xa[0] = zero
    xb[0] = zero
    xa[half + 1] = zero
    xb[half + 1] = zero
    even = lax.rem(lanes((HALO, WIDE)), 2) == 0

    def begin(q, _):
        for part, src in enumerate((lo, own, hi)):
            v = src[q]
            at = pl.ds(part * HALO, HALO)
            rhs[q, at] = jnp.where(even, v, pltpu.roll(v, 1, 1))
            diag[q, at] = jnp.where(even, pltpu.roll(v, WIDE - 1, 1), v) + 1.5
        d = rhs[q] * first
        step[q] = d
        xa[q + 1] = d
        return 0

    lax.fori_loop(0, half, begin, 0, unroll=True)
    old, new = xa, xb
    for damp, gain in pairs[: S_C - 1]:

        def sweep(q, _, old=old, new=new, damp=damp, gain=gain):
            v = old[q + 1]
            near = old[q] + old[q + 2] + lateral(v, 1, 2)
            resid = rhs[q] - diag[q] * v + 0.25 * near
            d = damp * step[q] + gain * resid
            step[q] = d
            new[q + 1] = v + d
            return 0

        lax.fori_loop(0, half, sweep, 0, unroll=True)
        old, new = new, old

    copy_r = lax.broadcasted_iota(jnp.int32, (rows, 2 * HALO), 0)
    copy_c = lax.broadcasted_iota(jnp.int32, (rows, 2 * HALO), 1)
    copy = jnp.where(lax.shift_right_logical(copy_r, 1) == copy_c, 1.0, 0.0).astype(F32)

    def refine(q, _):
        c = jnp.dot(copy, old[q + 1, HALO:, :MAIN], precision=lax.Precision.HIGHEST, preferred_element_type=F32)
        for j in range(2):
            adj[2 * q + j] = smooth[2 * q + j] + c
        return 0

    lax.fori_loop(0, half, refine, 0, unroll=True)
    adj[NR] = jnp.zeros((rows, MAIN), F32)
    for m, out in enumerate((o0, o1, o2, o3)):
        base = (ids[4] ^ m) * LAYERS
        for j in range(LAYERS + 1):
            out[2 * j] = adj[base + j, 0:8]
            out[2 * j + 1] = adj[base + j, 8:16]
        for j in range(LAYERS):
            out[2 * LAYERS + 2, pl.ds(j, 1)] = adj[base + j, 16:17]
        out[2 * LAYERS + 2, pl.ds(LAYERS, 4)] = jnp.zeros((4, MAIN), F32)


def gradient_kernel(ids, p0, p1, p2, p3, forward, forward_x, forward_r, viscosity, adjoint, gradient, above, beyond):
    for m, piece in enumerate((p0, p1, p2, p3)):
        at = pl.ds(pl.multiple_of(ids[m] * MAIN, 128), MAIN)
        for j in range(LAYERS):
            adjoint[j, 0:8, at] = piece[2 * j]
            adjoint[j, 8:16, at] = piece[2 * j + 1]
        above[0:8, at] = piece[2 * LAYERS]
        above[8:16, at] = piece[2 * LAYERS + 1]
        beyond[:, at] = piece[2 * LAYERS + 2]
    last = lax.broadcasted_iota(jnp.int32, (ROWS, 1024), 0) == ROWS - 1
    for j in range(LAYERS):
        a = adjoint[j]
        f = forward[j]
        a_r = (adjoint[j + 1] if j + 1 < LAYERS else above[...]) - a
        f_r = (forward[j + 1] if j + 1 < LAYERS else forward_r[0]) - f
        a_x = jnp.where(last, beyond[pl.ds(j, 1)], pltpu.roll(a, ROWS - 1, 0)) - a
        f_x = jnp.where(last, forward_x[j], pltpu.roll(f, ROWS - 1, 0)) - f
        a_y = pltpu.roll(a, 1023, 1) - a
        f_y = pltpu.roll(f, 1023, 1) - f
        gradient[j] = viscosity[j] * (f_r * a_r + f_x * a_x + f_y * a_y)


def struct(*shape):
    return jax.ShapeDtypeStruct(shape, F32)


def call(kernel, outs, scratch, ids, *args):
    whole = pl.BlockSpec(memory_space=pltpu.VMEM)
    return pl.pallas_call(
        kernel,
        out_shape=outs,
        in_specs=[pl.BlockSpec(memory_space=pltpu.SMEM)] + [whole] * len(args),
        out_specs=[whole] * len(outs),
        scratch_shapes=[pltpu.VMEM(s, F32) for s in scratch],
        compiler_params=VMEM,
    )(ids, *args)


def body(source, kappa, forward, viscosity):
    lat_n = lax.axis_size("lat")
    rad_n = lax.axis_size("rad")
    lat = lax.axis_index("lat")
    rad = lax.axis_index("rad")

    def flip(i):
        return ((i // 4) % 2) * 2

    turn = flip(lat)
    ids = jnp.stack([rad ^ turn, rad ^ 1 ^ turn, rad ^ 2 ^ turn, rad ^ 3 ^ turn, rad]).astype(jnp.int32)

    def trade(pieces):
        out = [pieces[0]]
        for m in range(1, rad_n):
            out.append(lax.ppermute(pieces[m], "rad", [(k, k ^ m) for k in range(rad_n)]))
        return out

    def beside(v, way):
        pairs = []
        for i in range(lat_n):
            to = (i + way) % lat_n
            for k in range(rad_n):
                pairs.append((i * rad_n + k, to * rad_n + (k ^ flip(i) ^ flip(to))))
        return lax.ppermute(v, ("lat", "rad"), pairs)

    slab = pltpu.VMEM((LAYERS, ROWS, 1024), F32)
    pieces = pl.pallas_call(
        pack_windows,
        out_shape=[struct(LAYERS, ROWS, PACKED)] * 4,
        in_specs=[pl.BlockSpec(memory_space=pltpu.SMEM)] + [pl.BlockSpec(memory_space=pltpu.HBM)] * 2,
        out_specs=[pl.BlockSpec(memory_space=pltpu.VMEM)] * 4,
        scratch_shapes=[slab, slab, pltpu.SemaphoreType.DMA((2, LAYERS))],
        compiler_params=VMEM,
    )(ids, source, kappa)
    pieces = trade(pieces)
    near, ahead = lax.optimization_barrier((pieces[1], forward))
    forward_x = lax.ppermute(ahead[:, :1], "lat", [((i + 1) % lat_n, i) for i in range(lat_n)])
    forward_r = lax.ppermute(ahead[:1], "rad", [(k + 1, k) for k in range(rad_n - 1)])
    forward_x, forward_r, *pieces = lax.optimization_barrier((forward_x, forward_r, pieces[0], near, *pieces[2:]))
    up, down = call(pack_rows, [struct(NR, HALO, PACKED)] * 2, [], ids, *pieces)
    lo = beside(up, 1)
    hi = beside(down, -1)
    deep = (NR, 2 * ROWS, WIDE)
    padded = (NR + 2, 2 * ROWS, WIDE)
    smooth, packed = call(
        fine_kernel,
        [struct(NR, 3 * HALO, MAIN), struct(NR // 2, HALO, WIDE)],
        [deep, deep, padded, padded, deep],
        ids,
        *pieces,
        lo,
        hi,
    )
    below = beside(packed, 1)
    over = beside(packed, -1)
    deep = (NR // 2, 3 * HALO, WIDE)
    padded = (NR // 2 + 2, 3 * HALO, WIDE)
    backs = call(
        coarse_kernel,
        [struct(2 * LAYERS + 3, 8, MAIN)] * 4,
        [deep, deep, padded, padded, deep, (NR + 1, 3 * HALO, MAIN)],
        ids,
        below,
        packed,
        over,
        smooth,
    )
    backs = trade(backs)
    adjoint, gradient = call(
        gradient_kernel,
        [struct(LAYERS, ROWS, 1024)] * 2,
        [(ROWS, 1024), (8, 1024)],
        ids,
        *backs,
        forward,
        forward_x,
        forward_r,
        viscosity,
    )
    return adjoint, gradient


def solution(mesh):
    placed = P("rad", "lat", None)
    return jax.shard_map(
        body,
        mesh=mesh,
        in_specs=(placed,) * 4,
        out_specs=(placed,) * 2,
        check_vma=False,
    )
```

```python
import jax
import jax.numpy as jnp
from jax import lax
from jax.experimental import pallas as pl
from jax.experimental.pallas import tpu as pltpu
from jax.sharding import PartitionSpec as P

S_F = 8
S_C = 8
FINE = (1.5, 12.5)
COARSE = (0.05, 3.5)

LAYERS = 4
ROWS = 16
NR = 16
HALO = 8
MAIN = 256
WIDE = 384
PACKED = 640
EDGE = 32
VMEM = pltpu.CompilerParams(vmem_limit_bytes=40 * 1024 * 1024)
F32 = jnp.float32


def lanes(shape):
    return lax.broadcasted_iota(jnp.int32, shape, len(shape) - 1)


def coefficients(low, high, sweeps):
    theta = (high + low) / 2.0
    delta = (high - low) / 2.0
    sigma = theta / delta
    rho = 1.0 / sigma
    pairs = []
    for _ in range(sweeps):
        rho_new = 1.0 / (2.0 * sigma - rho)
        pairs.append((rho_new * rho, 2.0 * rho_new / delta))
        rho = rho_new
    return 1.0 / theta, pairs


def pack_windows(ids, source_hbm, kappa_hbm, *refs):
    outs, (source, kappa, done) = refs[:4], refs[4:]
    loads = []
    for f, (src, dst) in enumerate(((source_hbm, source), (kappa_hbm, kappa))):
        for j in range(LAYERS):
            loads.append(pltpu.make_async_copy(src.at[j], dst.at[j], done.at[f, j]))
            loads[-1].start()
    for load in loads:
        load.wait()
    lane = lanes((LAYERS, ROWS, 128))
    right = lane < EDGE
    left = lane >= 128 - EDGE
    for m, out in enumerate(outs):
        base = ids[m] * MAIN
        main = pl.ds(pl.multiple_of(base, 128), MAIN)
        after = pl.ds(pl.multiple_of(lax.rem(base + MAIN, 1024), 128), 128)
        before = pl.ds(pl.multiple_of(lax.rem(base + 1024 - 128, 1024), 128), 128)
        out[:, :, 0:MAIN] = source[:, :, main]
        out[:, :, MAIN : 2 * MAIN] = kappa[:, :, main]
        edge_s = jnp.where(right, source[:, :, after], source[:, :, before])
        edge_k = jnp.where(right, kappa[:, :, after], kappa[:, :, before])
        edge_k = pltpu.roll(edge_k, 64, 2)
        out[:, :, 2 * MAIN :] = jnp.where(right | left, edge_s, edge_k)


def pack_rows(ids, p0, p1, p2, p3, near, far):
    near_rows = pl.ds(pl.multiple_of((1 - ids[5]) * HALO, HALO), HALO)
    far_rows = pl.ds(pl.multiple_of(ids[5] * HALO, HALO), HALO)
    for m, piece in enumerate((p0, p1, p2, p3)):
        at = pl.ds((ids[4] ^ m) * LAYERS, LAYERS)
        near[at] = piece[:, near_rows, :]
        far[at] = piece[:, far_rows, :]


def spread(packed, rhs, diag):
    lane = lanes(packed.shape[:-1] + (128,))
    keep = (lane < EDGE) | (lane >= 128 - EDGE)
    edge = packed[..., 2 * MAIN :]
    rhs_edge = jnp.where(keep, edge, 0.0)
    diag_edge = jnp.where(keep, pltpu.roll(edge, 64, edge.ndim - 1), 0.0)
    rhs[..., :MAIN] = packed[..., :MAIN]
    rhs[..., MAIN:] = rhs_edge
    diag[..., :MAIN] = packed[..., MAIN : 2 * MAIN] + 6.0
    diag[..., MAIN:] = diag_edge + 6.0


def lateral(v, step_x, step_y):
    rows, width = v.shape
    return (
        pltpu.roll(v, step_x, 0)
        + pltpu.roll(v, rows - step_x, 0)
        + pltpu.roll(v, step_y, 1)
        + pltpu.roll(v, width - step_y, 1)
    )


def fine_kernel(ids, p0, p1, p2, p3, near, far, packed, o0, o1, o2, o3, rhs, diag, xa, xb, step):
    me = ids[4]
    for m, piece in enumerate((p0, p1, p2, p3)):
        base = (me ^ m) * LAYERS

        def fill(j, _, piece=piece, base=base):
            own = pl.ds(HALO, ROWS)
            spread(piece[j], rhs.at[base + j, own], diag.at[base + j, own])
            return 0

        lax.fori_loop(0, LAYERS, fill, 0, unroll=True)

    near_at = pl.ds(pl.multiple_of((1 - ids[5]) * (HALO + ROWS), HALO), HALO)
    far_at = pl.ds(pl.multiple_of(ids[5] * (HALO + ROWS), HALO), HALO)
    first, pairs = coefficients(*FINE, S_F)
    zero = jnp.zeros((2 * ROWS, WIDE), F32)
    xa[0] = zero
    xb[0] = zero
    xa[NR + 1] = zero
    xb[NR + 1] = zero

    def begin(r, _):
        spread(near[r], rhs.at[r, near_at], diag.at[r, near_at])
        spread(far[r], rhs.at[r, far_at], diag.at[r, far_at])
        d = rhs[r] * first
        step[r] = d
        xa[r + 1] = d
        return 0

    lax.fori_loop(0, NR, begin, 0, unroll=True)

    old, new = xa, xb
    for damp, gain in pairs[: S_F - 1]:

        def sweep(r, _, old=old, new=new, damp=damp, gain=gain):
            v = old[r + 1]
            around = old[r] + old[r + 2] + lateral(v, 1, 1)
            resid = rhs[r] - diag[r] * v + around
            d = damp * step[r] + gain * resid
            step[r] = d
            new[r + 1] = v + d
            return 0

        lax.fori_loop(0, NR, sweep, 0, unroll=True)
        old, new = new, old

    even_row = lax.rem(lax.broadcasted_iota(jnp.int32, (ROWS, WIDE), 0), 2) == 0
    even_lane = lax.rem(lanes((HALO, WIDE)), 2) == 0
    pick_r = lax.broadcasted_iota(jnp.int32, (HALO, ROWS), 0)
    pick_c = lax.broadcasted_iota(jnp.int32, (HALO, ROWS), 1)
    pick = jnp.where(lax.shift_right_logical(pick_c, 1) == pick_r, 0.125, 0.0).astype(F32)

    def block_mean(v):
        s = jnp.dot(pick, v, precision=lax.Precision.HIGHEST, preferred_element_type=F32)
        return s + jnp.where(even_lane, pltpu.roll(s, WIDE - 1, 1), pltpu.roll(s, 1, 1))

    def residual(q, _):
        total = None
        diags = None
        for j in range(2):
            r = 2 * q + j
            v = old[r + 1]
            around = old[r] + old[r + 2] + lateral(v, 1, 1)
            resid = (rhs[r] - diag[r] * v + around)[HALO : HALO + ROWS]
            total = resid if total is None else total + resid
            k = diag[r, HALO : HALO + ROWS] - 6.0
            diags = k if diags is None else diags + k
        packed[q] = jnp.where(even_lane, block_mean(total), block_mean(diags))
        return 0

    lax.fori_loop(0, NR // 2, residual, 0, unroll=True)
    for m, out in enumerate((o0, o1, o2, o3)):
        base = (me ^ m) * LAYERS + 1
        for j in range(LAYERS + 1):
            for h in range(2):
                out[2 * j + h] = old[base + j, (1 + h) * HALO : (2 + h) * HALO, :MAIN]
        for j in range(LAYERS):
            out[2 * LAYERS + 2, pl.ds(j, 1)] = old[base + j, 3 * HALO : 3 * HALO + 1, :MAIN]
        out[2 * LAYERS + 2, pl.ds(LAYERS, 4)] = jnp.zeros((4, MAIN), F32)


def coarse_kernel(ids, near, own, far, o0, o1, o2, o3, rhs, diag, xa, xb, step):
    first, pairs = coefficients(*COARSE, S_C)
    half = NR // 2
    rows = 3 * HALO
    zero = jnp.zeros((rows, WIDE), F32)
    xa[0] = zero
    xb[0] = zero
    xa[half + 1] = zero
    xb[half + 1] = zero
    even = lax.rem(lanes((HALO, WIDE)), 2) == 0

    def begin(q, _):
        for part, src in (((1 - ids[5]) * 2, near), (1, own), (ids[5] * 2, far)):
            v = src[q]
            at = pl.ds(pl.multiple_of(part * HALO, HALO), HALO)
            rhs[q, at] = jnp.where(even, v, pltpu.roll(v, 1, 1))
            diag[q, at] = jnp.where(even, pltpu.roll(v, WIDE - 1, 1), v) + 1.5
        d = rhs[q] * first
        step[q] = d
        xa[q + 1] = d
        return 0

    lax.fori_loop(0, half, begin, 0, unroll=True)
    old, new = xa, xb
    for damp, gain in pairs[: S_C - 1]:

        def sweep(q, _, old=old, new=new, damp=damp, gain=gain):
            v = old[q + 1]
            around = old[q] + old[q + 2] + lateral(v, 1, 2)
            resid = rhs[q] - diag[q] * v + 0.25 * around
            d = damp * step[q] + gain * resid
            step[q] = d
            new[q + 1] = v + d
            return 0

        lax.fori_loop(0, half, sweep, 0, unroll=True)
        old, new = new, old

    even = even[:, :MAIN]
    top = lax.broadcasted_iota(jnp.int32, (HALO, MAIN), 0) == 0
    own_rows = slice(HALO, 2 * HALO)
    after = slice(2 * HALO, 2 * HALO + 1)
    for m, out in enumerate((o0, o1, o2, o3)):
        base = (ids[4] ^ m) * (LAYERS // 2) + 1
        a, b, c = (old[base + j, own_rows, :MAIN] for j in range(3))
        out[0] = jnp.where(even, a, b)
        out[1] = jnp.where(even, c, jnp.where(top, old[base, after, :MAIN], old[base + 1, after, :MAIN]))


def gradient_kernel(ids, *refs):
    smooths, fixes = refs[:4], refs[4:8]
    forward, forward_x, forward_r, viscosity, adjoint, gradient, above, beyond, fix = refs[8:]
    for m in range(4):
        at = pl.ds(pl.multiple_of(ids[m] * MAIN, 128), MAIN)
        fix[:, :, at] = fixes[m][...]
    even = lax.rem(lanes((HALO, 1024)), 2) == 0
    low, high = fix[0], fix[1]
    coarse = (
        jnp.where(even, low, pltpu.roll(low, 1, 1)),
        jnp.where(even, pltpu.roll(low, 1023, 1), low),
        jnp.where(even, high, pltpu.roll(high, 1, 1)),
    )
    rest = jnp.where(even, pltpu.roll(high, 1023, 1), high)
    copy_r = lax.broadcasted_iota(jnp.int32, (ROWS, HALO), 0)
    copy_c = lax.broadcasted_iota(jnp.int32, (ROWS, HALO), 1)
    copy = jnp.where(lax.shift_right_logical(copy_r, 1) == copy_c, 1.0, 0.0).astype(F32)
    for l, c in enumerate(coarse):
        c = jnp.dot(copy, c, precision=lax.Precision.HIGHEST, preferred_element_type=F32)
        for j in (2 * l, 2 * l + 1):
            if j < LAYERS:
                adjoint[j] = c
            elif j == LAYERS:
                above[...] = c
    for j in range(LAYERS):
        beyond[pl.ds(j, 1)] = rest[j // 2 : j // 2 + 1]
    for m in range(4):
        at = pl.ds(pl.multiple_of(ids[m] * MAIN, 128), MAIN)
        piece = smooths[m]
        for h in range(2):
            rows = slice(h * HALO, (h + 1) * HALO)
            for j in range(LAYERS):
                adjoint[j, rows, at] += piece[2 * j + h]
            above[rows, at] += piece[2 * LAYERS + h]
        beyond[0:LAYERS, at] += piece[2 * LAYERS + 2, 0:LAYERS]
    last = lax.broadcasted_iota(jnp.int32, (ROWS, 1024), 0) == ROWS - 1
    for j in range(LAYERS):
        a = adjoint[j]
        f = forward[j]
        a_r = (adjoint[j + 1] if j + 1 < LAYERS else above[...]) - a
        f_r = (forward[j + 1] if j + 1 < LAYERS else forward_r[0]) - f
        a_x = jnp.where(last, beyond[pl.ds(j, 1)], pltpu.roll(a, ROWS - 1, 0)) - a
        f_x = jnp.where(last, forward_x[j], pltpu.roll(f, ROWS - 1, 0)) - f
        a_y = pltpu.roll(a, 1023, 1) - a
        f_y = pltpu.roll(f, 1023, 1) - f
        gradient[j] = viscosity[j] * (f_r * a_r + f_x * a_x + f_y * a_y)


def struct(*shape):
    return jax.ShapeDtypeStruct(shape, F32)


def call(kernel, outs, scratch, ids, *args):
    whole = pl.BlockSpec(memory_space=pltpu.VMEM)
    return pl.pallas_call(
        kernel,
        out_shape=outs,
        in_specs=[pl.BlockSpec(memory_space=pltpu.SMEM)] + [whole] * len(args),
        out_specs=[whole] * len(outs),
        scratch_shapes=[pltpu.VMEM(s, F32) for s in scratch],
        compiler_params=VMEM,
    )(ids, *args)


def body(source, kappa, forward, viscosity):
    lat_n = lax.axis_size("lat")
    rad_n = lax.axis_size("rad")
    lat = lax.axis_index("lat")
    rad = lax.axis_index("rad")

    def flip(i):
        return ((i // 4) % 2) * 2

    turn = flip(lat)
    ids = [rad ^ turn, rad ^ 1 ^ turn, rad ^ 2 ^ turn, rad ^ 3 ^ turn, rad, lat % 2]
    ids = jnp.stack(ids).astype(jnp.int32)

    def trade(pieces):
        out = [pieces[0]]
        for m in range(1, rad_n):
            out.append(lax.ppermute(pieces[m], "rad", [(k, k ^ m) for k in range(rad_n)]))
        return out

    def beside(near, far):
        out = []
        for shift, v in ((1, far), (0, near)):
            pairs = []
            for i in range(lat_n):
                to = (((i + shift) ^ 1) - shift) % lat_n
                for k in range(rad_n):
                    pairs.append((i * rad_n + k, to * rad_n + (k ^ flip(i) ^ flip(to))))
            out.append(lax.ppermute(v, ("lat", "rad"), pairs))
        return out[1], out[0]

    slab = pltpu.VMEM((LAYERS, ROWS, 1024), F32)
    pieces = pl.pallas_call(
        pack_windows,
        out_shape=[struct(LAYERS, ROWS, PACKED)] * 4,
        in_specs=[pl.BlockSpec(memory_space=pltpu.SMEM)] + [pl.BlockSpec(memory_space=pltpu.HBM)] * 2,
        out_specs=[pl.BlockSpec(memory_space=pltpu.VMEM)] * 4,
        scratch_shapes=[slab, slab, pltpu.SemaphoreType.DMA((2, LAYERS))],
        compiler_params=pltpu.CompilerParams(vmem_limit_bytes=56 * 1024 * 1024),
    )(ids, source, kappa)
    pieces = trade(pieces)
    first, ahead = lax.optimization_barrier((pieces[1], forward))
    forward_x = lax.ppermute(ahead[:, :1], "lat", [((i + 1) % lat_n, i) for i in range(lat_n)])
    forward_r = lax.ppermute(ahead[:1], "rad", [(k + 1, k) for k in range(rad_n - 1)])
    forward_x, forward_r, *pieces = lax.optimization_barrier((forward_x, forward_r, pieces[0], first, *pieces[2:]))
    near, far = call(pack_rows, [struct(NR, HALO, PACKED)] * 2, [], ids, *pieces)
    near, far = beside(near, far)
    deep = (NR, 2 * ROWS, WIDE)
    padded = (NR + 2, 2 * ROWS, WIDE)
    packed, *smooths = call(
        fine_kernel,
        [struct(NR // 2, HALO, WIDE)] + [struct(2 * LAYERS + 3, HALO, MAIN)] * 4,
        [deep, deep, padded, padded, deep],
        ids,
        *pieces,
        near,
        far,
    )
    near, far = beside(packed, packed)
    near, *smooths = lax.optimization_barrier((near, *smooths))
    smooths = trade(smooths)
    deep = (NR // 2, 3 * HALO, WIDE)
    padded = (NR // 2 + 2, 3 * HALO, WIDE)
    fixes = call(
        coarse_kernel,
        [struct(2, HALO, MAIN)] * 4,
        [deep, deep, padded, padded, deep],
        ids,
        near,
        packed,
        far,
    )
    joined = lax.optimization_barrier((*smooths, *fixes))
    smooths, fixes = joined[:4], trade(joined[4:])
    adjoint, gradient = call(
        gradient_kernel,
        [struct(LAYERS, ROWS, 1024)] * 2,
        [(ROWS, 1024), (HALO, 1024), (2, HALO, 1024)],
        ids,
        *smooths,
        *fixes,
        forward,
        forward_x,
        forward_r,
        viscosity,
    )
    return adjoint, gradient


def solution(mesh):
    placed = P("rad", "lat", None)
    return jax.shard_map(
        body,
        mesh=mesh,
        in_specs=(placed,) * 4,
        out_specs=(placed,) * 2,
        check_vma=False,
    )
```

```python
import jax
import jax.numpy as jnp
from jax import lax
from jax.experimental import pallas as pl
from jax.experimental.pallas import tpu as pltpu
from jax.sharding import PartitionSpec as P

S_F = 8
S_C = 8
FINE = (1.5, 12.5)
COARSE = (0.05, 3.5)

LAYERS = 4
ROWS = 16
NR = 16
HALO = 8
MAIN = 256
WIDE = 384
PACKED = 640
EDGE = 32
VMEM = pltpu.CompilerParams(vmem_limit_bytes=40 * 1024 * 1024)
F32 = jnp.float32


def lanes(shape):
    return lax.broadcasted_iota(jnp.int32, shape, len(shape) - 1)


def coefficients(low, high, sweeps):
    theta = (high + low) / 2.0
    delta = (high - low) / 2.0
    sigma = theta / delta
    rho = 1.0 / sigma
    pairs = []
    for _ in range(sweeps):
        rho_new = 1.0 / (2.0 * sigma - rho)
        pairs.append((rho_new * rho, 2.0 * rho_new / delta))
        rho = rho_new
    return 1.0 / theta, pairs


def pack_windows(ids, source_hbm, kappa_hbm, *refs):
    outs, (source, kappa, done) = refs[:4], refs[4:]
    loads = []
    for f, (src, dst) in enumerate(((source_hbm, source), (kappa_hbm, kappa))):
        for j in range(LAYERS):
            loads.append(pltpu.make_async_copy(src.at[j], dst.at[j], done.at[f, j]))
            loads[-1].start()
    for load in loads:
        load.wait()
    lane = lanes((LAYERS, ROWS, 128))
    right = lane < EDGE
    left = lane >= 128 - EDGE
    for m, out in enumerate(outs):
        base = ids[m] * MAIN
        main = pl.ds(pl.multiple_of(base, 128), MAIN)
        after = pl.ds(pl.multiple_of(lax.rem(base + MAIN, 1024), 128), 128)
        before = pl.ds(pl.multiple_of(lax.rem(base + 1024 - 128, 1024), 128), 128)
        out[:, :, 0:MAIN] = source[:, :, main]
        out[:, :, MAIN : 2 * MAIN] = kappa[:, :, main]
        edge_s = jnp.where(right, source[:, :, after], source[:, :, before])
        edge_k = jnp.where(right, kappa[:, :, after], kappa[:, :, before])
        edge_k = pltpu.roll(edge_k, 64, 2)
        out[:, :, 2 * MAIN :] = jnp.where(right | left, edge_s, edge_k)


def pack_rows(ids, p0, p1, p2, p3, up, down):
    for m, piece in enumerate((p0, p1, p2, p3)):
        at = pl.ds((ids[4] ^ m) * LAYERS, LAYERS)
        up[at] = piece[:, HALO:, :]
        down[at] = piece[:, :HALO, :]


def spread(packed, rhs, diag):
    lane = lanes(packed.shape[:-1] + (128,))
    keep = (lane < EDGE) | (lane >= 128 - EDGE)
    edge = packed[..., 2 * MAIN :]
    rhs_edge = jnp.where(keep, edge, 0.0)
    diag_edge = jnp.where(keep, pltpu.roll(edge, 64, edge.ndim - 1), 0.0)
    rhs[..., :MAIN] = packed[..., :MAIN]
    rhs[..., MAIN:] = rhs_edge
    diag[..., :MAIN] = packed[..., MAIN : 2 * MAIN] + 6.0
    diag[..., MAIN:] = diag_edge + 6.0


def lateral(v, step_x, step_y):
    rows, width = v.shape
    return (
        pltpu.roll(v, step_x, 0)
        + pltpu.roll(v, rows - step_x, 0)
        + pltpu.roll(v, step_y, 1)
        + pltpu.roll(v, width - step_y, 1)
    )


def fine_kernel(ids, p0, p1, p2, p3, lo, hi, smooth, packed, rhs, diag, xa, xb, step):
    me = ids[4]
    for m, piece in enumerate((p0, p1, p2, p3)):
        base = (me ^ m) * LAYERS

        def fill(j, _, piece=piece, base=base):
            own = pl.ds(HALO, ROWS)
            spread(piece[j], rhs.at[base + j, own], diag.at[base + j, own])
            return 0

        lax.fori_loop(0, LAYERS, fill, 0, unroll=True)

    first, pairs = coefficients(*FINE, S_F)
    zero = jnp.zeros((2 * ROWS, WIDE), F32)
    xa[0] = zero
    xb[0] = zero
    xa[NR + 1] = zero
    xb[NR + 1] = zero

    def begin(r, _):
        spread(lo[r], rhs.at[r, pl.ds(0, HALO)], diag.at[r, pl.ds(0, HALO)])
        top = pl.ds(HALO + ROWS, HALO)
        spread(hi[r], rhs.at[r, top], diag.at[r, top])
        d = rhs[r] * first
        step[r] = d
        xa[r + 1] = d
        return 0

    lax.fori_loop(0, NR, begin, 0, unroll=True)

    old, new = xa, xb
    for damp, gain in pairs[: S_F - 1]:

        def sweep(r, _, old=old, new=new, damp=damp, gain=gain):
            v = old[r + 1]
            near = old[r] + old[r + 2] + lateral(v, 1, 1)
            resid = rhs[r] - diag[r] * v + near
            d = damp * step[r] + gain * resid
            step[r] = d
            new[r + 1] = v + d
            return 0

        lax.fori_loop(0, NR, sweep, 0, unroll=True)
        old, new = new, old

    even_row = lax.rem(lax.broadcasted_iota(jnp.int32, (ROWS, WIDE), 0), 2) == 0
    even_lane = lax.rem(lanes((HALO, WIDE)), 2) == 0
    pick_r = lax.broadcasted_iota(jnp.int32, (HALO, ROWS), 0)
    pick_c = lax.broadcasted_iota(jnp.int32, (HALO, ROWS), 1)
    pick = jnp.where(lax.shift_right_logical(pick_c, 1) == pick_r, 0.125, 0.0).astype(F32)

    def block_mean(v):
        s = jnp.dot(pick, v, precision=lax.Precision.HIGHEST, preferred_element_type=F32)
        return s + jnp.where(even_lane, pltpu.roll(s, WIDE - 1, 1), pltpu.roll(s, 1, 1))

    def residual(q, _):
        total = None
        diags = None
        for j in range(2):
            r = 2 * q + j
            v = old[r + 1]
            near = old[r] + old[r + 2] + lateral(v, 1, 1)
            resid = (rhs[r] - diag[r] * v + near)[HALO : HALO + ROWS]
            total = resid if total is None else total + resid
            k = diag[r, HALO : HALO + ROWS] - 6.0
            diags = k if diags is None else diags + k
            smooth[r] = v[HALO:, :MAIN]
        packed[q] = jnp.where(even_lane, block_mean(total), block_mean(diags))
        return 0

    lax.fori_loop(0, NR // 2, residual, 0, unroll=True)


def coarse_kernel(ids, near, own, far, smooth, o0, o1, o2, o3, rhs, diag, xa, xb, step, adj):
    first, pairs = coefficients(*COARSE, S_C)
    half = NR // 2
    rows = 3 * HALO
    zero = jnp.zeros((rows, WIDE), F32)
    xa[0] = zero
    xb[0] = zero
    xa[half + 1] = zero
    xb[half + 1] = zero
    even = lax.rem(lanes((HALO, WIDE)), 2) == 0

    def begin(q, _):
        for part, src in (((1 - ids[5]) * 2, near), (1, own), (ids[5] * 2, far)):
            v = src[q]
            at = pl.ds(pl.multiple_of(part * HALO, HALO), HALO)
            rhs[q, at] = jnp.where(even, v, pltpu.roll(v, 1, 1))
            diag[q, at] = jnp.where(even, pltpu.roll(v, WIDE - 1, 1), v) + 1.5
        d = rhs[q] * first
        step[q] = d
        xa[q + 1] = d
        return 0

    lax.fori_loop(0, half, begin, 0, unroll=True)
    old, new = xa, xb
    for damp, gain in pairs[: S_C - 1]:

        def sweep(q, _, old=old, new=new, damp=damp, gain=gain):
            v = old[q + 1]
            around = old[q] + old[q + 2] + lateral(v, 1, 2)
            resid = rhs[q] - diag[q] * v + 0.25 * around
            d = damp * step[q] + gain * resid
            step[q] = d
            new[q + 1] = v + d
            return 0

        lax.fori_loop(0, half, sweep, 0, unroll=True)
        old, new = new, old

    copy_r = lax.broadcasted_iota(jnp.int32, (rows, 2 * HALO), 0)
    copy_c = lax.broadcasted_iota(jnp.int32, (rows, 2 * HALO), 1)
    copy = jnp.where(lax.shift_right_logical(copy_r, 1) == copy_c, 1.0, 0.0).astype(F32)

    def refine(q, _):
        c = jnp.dot(copy, old[q + 1, HALO:, :MAIN], precision=lax.Precision.HIGHEST, preferred_element_type=F32)
        for j in range(2):
            adj[2 * q + j] = smooth[2 * q + j] + c
        return 0

    lax.fori_loop(0, half, refine, 0, unroll=True)
    adj[NR] = jnp.zeros((rows, MAIN), F32)
    for m, out in enumerate((o0, o1, o2, o3)):
        base = (ids[4] ^ m) * LAYERS
        for j in range(LAYERS + 1):
            out[2 * j] = adj[base + j, 0:8]
            out[2 * j + 1] = adj[base + j, 8:16]
        for j in range(LAYERS):
            out[2 * LAYERS + 2, pl.ds(j, 1)] = adj[base + j, 16:17]
        out[2 * LAYERS + 2, pl.ds(LAYERS, 4)] = jnp.zeros((4, MAIN), F32)


def gradient_kernel(ids, p0, p1, p2, p3, forward, forward_x, forward_r, viscosity, adjoint, gradient, above, beyond):
    for m, piece in enumerate((p0, p1, p2, p3)):
        at = pl.ds(pl.multiple_of(ids[m] * MAIN, 128), MAIN)
        for j in range(LAYERS):
            adjoint[j, 0:8, at] = piece[2 * j]
            adjoint[j, 8:16, at] = piece[2 * j + 1]
        above[0:8, at] = piece[2 * LAYERS]
        above[8:16, at] = piece[2 * LAYERS + 1]
        beyond[:, at] = piece[2 * LAYERS + 2]
    last = lax.broadcasted_iota(jnp.int32, (ROWS, 1024), 0) == ROWS - 1
    for j in range(LAYERS):
        a = adjoint[j]
        f = forward[j]
        a_r = (adjoint[j + 1] if j + 1 < LAYERS else above[...]) - a
        f_r = (forward[j + 1] if j + 1 < LAYERS else forward_r[0]) - f
        a_x = jnp.where(last, beyond[pl.ds(j, 1)], pltpu.roll(a, ROWS - 1, 0)) - a
        f_x = jnp.where(last, forward_x[j], pltpu.roll(f, ROWS - 1, 0)) - f
        a_y = pltpu.roll(a, 1023, 1) - a
        f_y = pltpu.roll(f, 1023, 1) - f
        gradient[j] = viscosity[j] * (f_r * a_r + f_x * a_x + f_y * a_y)


def struct(*shape):
    return jax.ShapeDtypeStruct(shape, F32)


def call(kernel, outs, scratch, ids, *args):
    whole = pl.BlockSpec(memory_space=pltpu.VMEM)
    return pl.pallas_call(
        kernel,
        out_shape=outs,
        in_specs=[pl.BlockSpec(memory_space=pltpu.SMEM)] + [whole] * len(args),
        out_specs=[whole] * len(outs),
        scratch_shapes=[pltpu.VMEM(s, F32) for s in scratch],
        compiler_params=VMEM,
    )(ids, *args)


def body(source, kappa, forward, viscosity):
    lat_n = lax.axis_size("lat")
    rad_n = lax.axis_size("rad")
    lat = lax.axis_index("lat")
    rad = lax.axis_index("rad")

    def flip(i):
        return ((i // 4) % 2) * 2

    turn = flip(lat)
    ids = [rad ^ turn, rad ^ 1 ^ turn, rad ^ 2 ^ turn, rad ^ 3 ^ turn, rad, lat % 2]
    ids = jnp.stack(ids).astype(jnp.int32)

    def trade(pieces):
        out = [pieces[0]]
        for m in range(1, rad_n):
            out.append(lax.ppermute(pieces[m], "rad", [(k, k ^ m) for k in range(rad_n)]))
        return out

    def beside(v, way):
        pairs = []
        for i in range(lat_n):
            to = (i + way) % lat_n
            for k in range(rad_n):
                pairs.append((i * rad_n + k, to * rad_n + (k ^ flip(i) ^ flip(to))))
        return lax.ppermute(v, ("lat", "rad"), pairs)

    def swaps(near, far):
        out = []
        for shift, v in ((1, far), (0, near)):
            pairs = []
            for i in range(lat_n):
                to = (((i + shift) ^ 1) - shift) % lat_n
                for k in range(rad_n):
                    pairs.append((i * rad_n + k, to * rad_n + (k ^ flip(i) ^ flip(to))))
            out.append(lax.ppermute(v, ("lat", "rad"), pairs))
        return out[1], out[0]

    slab = pltpu.VMEM((LAYERS, ROWS, 1024), F32)
    pieces = pl.pallas_call(
        pack_windows,
        out_shape=[struct(LAYERS, ROWS, PACKED)] * 4,
        in_specs=[pl.BlockSpec(memory_space=pltpu.SMEM)] + [pl.BlockSpec(memory_space=pltpu.HBM)] * 2,
        out_specs=[pl.BlockSpec(memory_space=pltpu.VMEM)] * 4,
        scratch_shapes=[slab, slab, pltpu.SemaphoreType.DMA((2, LAYERS))],
        compiler_params=VMEM,
    )(ids, source, kappa)
    pieces = trade(pieces)
    near, ahead = lax.optimization_barrier((pieces[1], forward))
    forward_x = lax.ppermute(ahead[:, :1], "lat", [((i + 1) % lat_n, i) for i in range(lat_n)])
    forward_r = lax.ppermute(ahead[:1], "rad", [(k + 1, k) for k in range(rad_n - 1)])
    forward_x, forward_r, *pieces = lax.optimization_barrier((forward_x, forward_r, pieces[0], near, *pieces[2:]))
    up, down = call(pack_rows, [struct(NR, HALO, PACKED)] * 2, [], ids, *pieces)
    lo = beside(up, 1)
    hi = beside(down, -1)
    deep = (NR, 2 * ROWS, WIDE)
    padded = (NR + 2, 2 * ROWS, WIDE)
    smooth, packed = call(
        fine_kernel,
        [struct(NR, 3 * HALO, MAIN), struct(NR // 2, HALO, WIDE)],
        [deep, deep, padded, padded, deep],
        ids,
        *pieces,
        lo,
        hi,
    )
    near, far = swaps(packed, packed)
    deep = (NR // 2, 3 * HALO, WIDE)
    padded = (NR // 2 + 2, 3 * HALO, WIDE)
    backs = call(
        coarse_kernel,
        [struct(2 * LAYERS + 3, 8, MAIN)] * 4,
        [deep, deep, padded, padded, deep, (NR + 1, 3 * HALO, MAIN)],
        ids,
        near,
        packed,
        far,
        smooth,
    )
    backs = trade(backs)
    adjoint, gradient = call(
        gradient_kernel,
        [struct(LAYERS, ROWS, 1024)] * 2,
        [(ROWS, 1024), (8, 1024)],
        ids,
        *backs,
        forward,
        forward_x,
        forward_r,
        viscosity,
    )
    return adjoint, gradient


def solution(mesh):
    placed = P("rad", "lat", None)
    return jax.shard_map(
        body,
        mesh=mesh,
        in_specs=(placed,) * 4,
        out_specs=(placed,) * 2,
        check_vma=False,
    )
```

```python
import jax
import jax.numpy as jnp
from jax import lax
from jax.experimental import pallas as pl
from jax.experimental.pallas import tpu as pltpu
from jax.sharding import PartitionSpec as P

S_F = 8
S_C = 8
FINE = (1.5, 12.5)
COARSE = (0.05, 3.5)

LAYERS = 4
ROWS = 16
NR = 16
HALO = 8
MAIN = 256
WIDE = 384
PACKED = 640
EDGE = 32
VMEM = pltpu.CompilerParams(vmem_limit_bytes=40 * 1024 * 1024)
F32 = jnp.float32


def lanes(shape):
    return lax.broadcasted_iota(jnp.int32, shape, len(shape) - 1)


def coefficients(low, high, sweeps):
    theta = (high + low) / 2.0
    delta = (high - low) / 2.0
    sigma = theta / delta
    rho = 1.0 / sigma
    pairs = []
    for _ in range(sweeps):
        rho_new = 1.0 / (2.0 * sigma - rho)
        pairs.append((rho_new * rho, 2.0 * rho_new / delta))
        rho = rho_new
    return 1.0 / theta, pairs


def pack_windows(ids, source_hbm, kappa_hbm, *refs):
    outs, (source, kappa, done) = refs[:4], refs[4:]
    loads = []
    for f, (src, dst) in enumerate(((source_hbm, source), (kappa_hbm, kappa))):
        for j in range(LAYERS):
            loads.append(pltpu.make_async_copy(src.at[j], dst.at[j], done.at[f, j]))
            loads[-1].start()
    lane = lanes((ROWS, 128))
    right = lane < EDGE
    left = lane >= 128 - EDGE
    for j in range(LAYERS):
        loads[j].wait()
        loads[LAYERS + j].wait()
        for m, out in enumerate(outs):
            base = ids[m] * MAIN
            main = pl.ds(pl.multiple_of(base, 128), MAIN)
            after = pl.ds(pl.multiple_of(lax.rem(base + MAIN, 1024), 128), 128)
            before = pl.ds(pl.multiple_of(lax.rem(base + 1024 - 128, 1024), 128), 128)
            out[j, :, 0:MAIN] = source[j, :, main]
            out[j, :, MAIN : 2 * MAIN] = kappa[j, :, main]
            edge_s = jnp.where(right, source[j, :, after], source[j, :, before])
            edge_k = jnp.where(right, kappa[j, :, after], kappa[j, :, before])
            edge_k = pltpu.roll(edge_k, 64, 1)
            out[j, :, 2 * MAIN :] = jnp.where(right | left, edge_s, edge_k)


def pack_rows(ids, p0, p1, p2, p3, up, down):
    for m, piece in enumerate((p0, p1, p2, p3)):
        at = pl.ds((ids[4] ^ m) * LAYERS, LAYERS)
        up[at] = piece[:, HALO:, :]
        down[at] = piece[:, :HALO, :]


def spread(packed, rhs, diag):
    lane = lanes(packed.shape[:-1] + (128,))
    keep = (lane < EDGE) | (lane >= 128 - EDGE)
    edge = packed[..., 2 * MAIN :]
    rhs_edge = jnp.where(keep, edge, 0.0)
    diag_edge = jnp.where(keep, pltpu.roll(edge, 64, edge.ndim - 1), 0.0)
    rhs[..., :MAIN] = packed[..., :MAIN]
    rhs[..., MAIN:] = rhs_edge
    diag[..., :MAIN] = packed[..., MAIN : 2 * MAIN] + 6.0
    diag[..., MAIN:] = diag_edge + 6.0


def lateral(v, step_x, step_y):
    rows, width = v.shape
    return (
        pltpu.roll(v, step_x, 0)
        + pltpu.roll(v, rows - step_x, 0)
        + pltpu.roll(v, step_y, 1)
        + pltpu.roll(v, width - step_y, 1)
    )


def fine_kernel(ids, p0, p1, p2, p3, lo, hi, smooth, packed, rhs, diag, xa, xb, step):
    me = ids[4]
    for m, piece in enumerate((p0, p1, p2, p3)):
        base = (me ^ m) * LAYERS

        def fill(j, _, piece=piece, base=base):
            own = pl.ds(HALO, ROWS)
            spread(piece[j], rhs.at[base + j, own], diag.at[base + j, own])
            return 0

        lax.fori_loop(0, LAYERS, fill, 0, unroll=True)

    first, pairs = coefficients(*FINE, S_F)
    zero = jnp.zeros((2 * ROWS, WIDE), F32)
    xa[0] = zero
    xb[0] = zero
    xa[NR + 1] = zero
    xb[NR + 1] = zero

    def begin(r, _):
        spread(lo[r], rhs.at[r, pl.ds(0, HALO)], diag.at[r, pl.ds(0, HALO)])
        top = pl.ds(HALO + ROWS, HALO)
        spread(hi[r], rhs.at[r, top], diag.at[r, top])
        d = rhs[r] * first
        step[r] = d
        xa[r + 1] = d
        return 0

    lax.fori_loop(0, NR, begin, 0, unroll=True)

    old, new = xa, xb
    for damp, gain in pairs[: S_F - 1]:

        def sweep(r, _, old=old, new=new, damp=damp, gain=gain):
            v = old[r + 1]
            near = old[r] + old[r + 2] + lateral(v, 1, 1)
            resid = rhs[r] - diag[r] * v + near
            d = damp * step[r] + gain * resid
            step[r] = d
            new[r + 1] = v + d
            return 0

        lax.fori_loop(0, NR, sweep, 0, unroll=True)
        old, new = new, old

    even_row = lax.rem(lax.broadcasted_iota(jnp.int32, (ROWS, WIDE), 0), 2) == 0
    even_lane = lax.rem(lanes((HALO, WIDE)), 2) == 0
    pick_r = lax.broadcasted_iota(jnp.int32, (HALO, ROWS), 0)
    pick_c = lax.broadcasted_iota(jnp.int32, (HALO, ROWS), 1)
    pick = jnp.where(lax.shift_right_logical(pick_c, 1) == pick_r, 0.125, 0.0).astype(F32)

    def block_mean(v):
        s = jnp.dot(pick, v, precision=lax.Precision.HIGHEST, preferred_element_type=F32)
        return s + jnp.where(even_lane, pltpu.roll(s, WIDE - 1, 1), pltpu.roll(s, 1, 1))

    def residual(q, _):
        total = None
        diags = None
        for j in range(2):
            r = 2 * q + j
            v = old[r + 1]
            near = old[r] + old[r + 2] + lateral(v, 1, 1)
            resid = (rhs[r] - diag[r] * v + near)[HALO : HALO + ROWS]
            total = resid if total is None else total + resid
            k = diag[r, HALO : HALO + ROWS] - 6.0
            diags = k if diags is None else diags + k
            smooth[r] = v[HALO:, :MAIN]
        packed[q] = jnp.where(even_lane, block_mean(total), block_mean(diags))
        return 0

    lax.fori_loop(0, NR // 2, residual, 0, unroll=True)


def coarse_kernel(ids, near, own, far, smooth, o0, o1, o2, o3, rhs, diag, xa, xb, step, adj):
    first, pairs = coefficients(*COARSE, S_C)
    half = NR // 2
    rows = 3 * HALO
    zero = jnp.zeros((rows, WIDE), F32)
    xa[0] = zero
    xb[0] = zero
    xa[half + 1] = zero
    xb[half + 1] = zero
    even = lax.rem(lanes((HALO, WIDE)), 2) == 0

    def begin(q, _):
        for part, src in (((1 - ids[5]) * 2, near), (1, own), (ids[5] * 2, far)):
            v = src[q]
            at = pl.ds(pl.multiple_of(part * HALO, HALO), HALO)
            rhs[q, at] = jnp.where(even, v, pltpu.roll(v, 1, 1))
            diag[q, at] = jnp.where(even, pltpu.roll(v, WIDE - 1, 1), v) + 1.5
        d = rhs[q] * first
        step[q] = d
        xa[q + 1] = d
        return 0

    lax.fori_loop(0, half, begin, 0, unroll=True)
    old, new = xa, xb
    for damp, gain in pairs[: S_C - 1]:

        def sweep(q, _, old=old, new=new, damp=damp, gain=gain):
            v = old[q + 1]
            around = old[q] + old[q + 2] + lateral(v, 1, 2)
            resid = rhs[q] - diag[q] * v + 0.25 * around
            d = damp * step[q] + gain * resid
            step[q] = d
            new[q + 1] = v + d
            return 0

        lax.fori_loop(0, half, sweep, 0, unroll=True)
        old, new = new, old

    copy_r = lax.broadcasted_iota(jnp.int32, (rows, 2 * HALO), 0)
    copy_c = lax.broadcasted_iota(jnp.int32, (rows, 2 * HALO), 1)
    copy = jnp.where(lax.shift_right_logical(copy_r, 1) == copy_c, 1.0, 0.0).astype(F32)

    def refine(q, _):
        c = jnp.dot(copy, old[q + 1, HALO:, :MAIN], precision=lax.Precision.HIGHEST, preferred_element_type=F32)
        for j in range(2):
            adj[2 * q + j] = smooth[2 * q + j] + c
        return 0

    lax.fori_loop(0, half, refine, 0, unroll=True)
    adj[NR] = jnp.zeros((rows, MAIN), F32)
    for m, out in enumerate((o0, o1, o2, o3)):
        base = (ids[4] ^ m) * LAYERS
        for j in range(LAYERS + 1):
            out[2 * j] = adj[base + j, 0:8]
            out[2 * j + 1] = adj[base + j, 8:16]
        for j in range(LAYERS):
            out[2 * LAYERS + 2, pl.ds(j, 1)] = adj[base + j, 16:17]
        out[2 * LAYERS + 2, pl.ds(LAYERS, 4)] = jnp.zeros((4, MAIN), F32)


def gradient_kernel(ids, p0, p1, p2, p3, forward, forward_x, forward_r, viscosity, adjoint, gradient, above, beyond):
    for m, piece in enumerate((p0, p1, p2, p3)):
        at = pl.ds(pl.multiple_of(ids[m] * MAIN, 128), MAIN)
        for j in range(LAYERS):
            adjoint[j, 0:8, at] = piece[2 * j]
            adjoint[j, 8:16, at] = piece[2 * j + 1]
        above[0:8, at] = piece[2 * LAYERS]
        above[8:16, at] = piece[2 * LAYERS + 1]
        beyond[:, at] = piece[2 * LAYERS + 2]
    last = lax.broadcasted_iota(jnp.int32, (ROWS, 1024), 0) == ROWS - 1
    for j in range(LAYERS):
        a = adjoint[j]
        f = forward[j]
        a_r = (adjoint[j + 1] if j + 1 < LAYERS else above[...]) - a
        f_r = (forward[j + 1] if j + 1 < LAYERS else forward_r[0]) - f
        a_x = jnp.where(last, beyond[pl.ds(j, 1)], pltpu.roll(a, ROWS - 1, 0)) - a
        f_x = jnp.where(last, forward_x[j], pltpu.roll(f, ROWS - 1, 0)) - f
        a_y = pltpu.roll(a, 1023, 1) - a
        f_y = pltpu.roll(f, 1023, 1) - f
        gradient[j] = viscosity[j] * (f_r * a_r + f_x * a_x + f_y * a_y)


def struct(*shape):
    return jax.ShapeDtypeStruct(shape, F32)


def call(kernel, outs, scratch, ids, *args):
    whole = pl.BlockSpec(memory_space=pltpu.VMEM)
    return pl.pallas_call(
        kernel,
        out_shape=outs,
        in_specs=[pl.BlockSpec(memory_space=pltpu.SMEM)] + [whole] * len(args),
        out_specs=[whole] * len(outs),
        scratch_shapes=[pltpu.VMEM(s, F32) for s in scratch],
        compiler_params=VMEM,
    )(ids, *args)


def body(source, kappa, forward, viscosity):
    lat_n = lax.axis_size("lat")
    rad_n = lax.axis_size("rad")
    lat = lax.axis_index("lat")
    rad = lax.axis_index("rad")

    def flip(i):
        return ((i // 4) % 2) * 2

    turn = flip(lat)
    ids = [rad ^ turn, rad ^ 1 ^ turn, rad ^ 2 ^ turn, rad ^ 3 ^ turn, rad, lat % 2]
    ids = jnp.stack(ids).astype(jnp.int32)

    def trade(pieces):
        out = [pieces[0]]
        for m in range(1, rad_n):
            out.append(lax.ppermute(pieces[m], "rad", [(k, k ^ m) for k in range(rad_n)]))
        return out

    def beside(v, way):
        pairs = []
        for i in range(lat_n):
            to = (i + way) % lat_n
            for k in range(rad_n):
                pairs.append((i * rad_n + k, to * rad_n + (k ^ flip(i) ^ flip(to))))
        return lax.ppermute(v, ("lat", "rad"), pairs)

    def swaps(near, far):
        out = []
        for shift, v in ((1, far), (0, near)):
            pairs = []
            for i in range(lat_n):
                to = (((i + shift) ^ 1) - shift) % lat_n
                for k in range(rad_n):
                    pairs.append((i * rad_n + k, to * rad_n + (k ^ flip(i) ^ flip(to))))
            out.append(lax.ppermute(v, ("lat", "rad"), pairs))
        return out[1], out[0]

    slab = pltpu.VMEM((LAYERS, ROWS, 1024), F32)
    pieces = pl.pallas_call(
        pack_windows,
        out_shape=[struct(LAYERS, ROWS, PACKED)] * 4,
        in_specs=[pl.BlockSpec(memory_space=pltpu.SMEM)] + [pl.BlockSpec(memory_space=pltpu.HBM)] * 2,
        out_specs=[pl.BlockSpec(memory_space=pltpu.VMEM)] * 4,
        scratch_shapes=[slab, slab, pltpu.SemaphoreType.DMA((2, LAYERS))],
        compiler_params=VMEM,
    )(ids, pltpu.with_memory_space_constraint(source, pltpu.HBM), pltpu.with_memory_space_constraint(kappa, pltpu.HBM))
    pieces = trade(pieces)
    near, ahead = lax.optimization_barrier((pieces[1], forward))
    forward_x = lax.ppermute(ahead[:, :1], "lat", [((i + 1) % lat_n, i) for i in range(lat_n)])
    forward_r = lax.ppermute(ahead[:1], "rad", [(k + 1, k) for k in range(rad_n - 1)])
    forward_x, forward_r, *pieces = lax.optimization_barrier((forward_x, forward_r, pieces[0], near, *pieces[2:]))
    up, down = call(pack_rows, [struct(NR, HALO, PACKED)] * 2, [], ids, *pieces)
    lo = beside(up, 1)
    hi = beside(down, -1)
    deep = (NR, 2 * ROWS, WIDE)
    padded = (NR + 2, 2 * ROWS, WIDE)
    smooth, packed = call(
        fine_kernel,
        [struct(NR, 3 * HALO, MAIN), struct(NR // 2, HALO, WIDE)],
        [deep, deep, padded, padded, deep],
        ids,
        *pieces,
        lo,
        hi,
    )
    near, far = swaps(packed, packed)
    deep = (NR // 2, 3 * HALO, WIDE)
    padded = (NR // 2 + 2, 3 * HALO, WIDE)
    backs = call(
        coarse_kernel,
        [struct(2 * LAYERS + 3, 8, MAIN)] * 4,
        [deep, deep, padded, padded, deep, (NR + 1, 3 * HALO, MAIN)],
        ids,
        near,
        packed,
        far,
        smooth,
    )
    backs = trade(backs)
    adjoint, gradient = call(
        gradient_kernel,
        [struct(LAYERS, ROWS, 1024)] * 2,
        [(ROWS, 1024), (8, 1024)],
        ids,
        *backs,
        forward,
        forward_x,
        forward_r,
        viscosity,
    )
    return adjoint, gradient


def solution(mesh):
    placed = P("rad", "lat", None)
    return jax.shard_map(
        body,
        mesh=mesh,
        in_specs=(placed,) * 4,
        out_specs=(placed,) * 2,
        check_vma=False,
    )
```

```python
import jax
import jax.numpy as jnp
from jax import lax
from jax.experimental import pallas as pl
from jax.experimental.pallas import tpu as pltpu
from jax.sharding import PartitionSpec as P

S_F = 8
S_C = 8
FINE = (1.5, 12.5)
COARSE = (0.05, 3.5)

LAYERS = 4
ROWS = 16
NR = 16
HALO = 8
MAIN = 256
WIDE = 384
PACKED = 640
EDGE = 32
VMEM = pltpu.CompilerParams(vmem_limit_bytes=40 * 1024 * 1024)
F32 = jnp.float32


def lanes(shape):
    return lax.broadcasted_iota(jnp.int32, shape, len(shape) - 1)


def coefficients(low, high, sweeps):
    theta = (high + low) / 2.0
    delta = (high - low) / 2.0
    sigma = theta / delta
    rho = 1.0 / sigma
    pairs = []
    for _ in range(sweeps):
        rho_new = 1.0 / (2.0 * sigma - rho)
        pairs.append((rho_new * rho, 2.0 * rho_new / delta))
        rho = rho_new
    return 1.0 / theta, pairs


def pack_windows(ids, source_hbm, kappa_hbm, *refs):
    outs, (source, kappa, done) = refs[:4], refs[4:]
    loads = []
    for f, (src, dst) in enumerate(((source_hbm, source), (kappa_hbm, kappa))):
        for j in range(LAYERS):
            loads.append(pltpu.make_async_copy(src.at[j], dst.at[j], done.at[f, j]))
            loads[-1].start()
    lane = lanes((ROWS, 128))
    right = lane < EDGE
    left = lane >= 128 - EDGE
    for j in range(LAYERS):
        loads[j].wait()
        loads[LAYERS + j].wait()
        for m, out in enumerate(outs):
            base = ids[m] * MAIN
            main = pl.ds(pl.multiple_of(base, 128), MAIN)
            after = pl.ds(pl.multiple_of(lax.rem(base + MAIN, 1024), 128), 128)
            before = pl.ds(pl.multiple_of(lax.rem(base + 1024 - 128, 1024), 128), 128)
            out[j, :, 0:MAIN] = source[j, :, main]
            out[j, :, MAIN : 2 * MAIN] = kappa[j, :, main]
            edge_s = jnp.where(right, source[j, :, after], source[j, :, before])
            edge_k = jnp.where(right, kappa[j, :, after], kappa[j, :, before])
            edge_k = pltpu.roll(edge_k, 64, 1)
            out[j, :, 2 * MAIN :] = jnp.where(right | left, edge_s, edge_k)


def pack_rows(ids, p0, p1, p2, p3, up, down):
    for m, piece in enumerate((p0, p1, p2, p3)):
        at = pl.ds((ids[4] ^ m) * LAYERS, LAYERS)
        up[at] = piece[:, HALO:, :]
        down[at] = piece[:, :HALO, :]


def spread(packed, rhs, diag):
    lane = lanes(packed.shape[:-1] + (128,))
    keep = (lane < EDGE) | (lane >= 128 - EDGE)
    edge = packed[..., 2 * MAIN :]
    rhs_edge = jnp.where(keep, edge, 0.0)
    diag_edge = jnp.where(keep, pltpu.roll(edge, 64, edge.ndim - 1), 0.0)
    rhs[..., :MAIN] = packed[..., :MAIN]
    rhs[..., MAIN:] = rhs_edge
    diag[..., :MAIN] = packed[..., MAIN : 2 * MAIN] + 6.0
    diag[..., MAIN:] = diag_edge + 6.0


def lateral(v, step_x, step_y):
    rows, width = v.shape
    return (
        pltpu.roll(v, step_x, 0)
        + pltpu.roll(v, rows - step_x, 0)
        + pltpu.roll(v, step_y, 1)
        + pltpu.roll(v, width - step_y, 1)
    )


def fine_kernel(ids, p0, p1, p2, p3, lo, hi, smooth, packed, rhs, diag, xa, xb, step):
    me = ids[4]
    for m, piece in enumerate((p0, p1, p2, p3)):
        base = (me ^ m) * LAYERS

        def fill(j, _, piece=piece, base=base):
            own = pl.ds(HALO, ROWS)
            spread(piece[j], rhs.at[base + j, own], diag.at[base + j, own])
            return 0

        lax.fori_loop(0, LAYERS, fill, 0, unroll=True)

    first, pairs = coefficients(*FINE, S_F)
    zero = jnp.zeros((2 * ROWS, WIDE), F32)
    xa[0] = zero
    xb[0] = zero
    xa[NR + 1] = zero
    xb[NR + 1] = zero

    def begin(r, _):
        spread(lo[r], rhs.at[r, pl.ds(0, HALO)], diag.at[r, pl.ds(0, HALO)])
        top = pl.ds(HALO + ROWS, HALO)
        spread(hi[r], rhs.at[r, top], diag.at[r, top])
        d = rhs[r] * first
        step[r] = d
        xa[r + 1] = d
        return 0

    lax.fori_loop(0, NR, begin, 0, unroll=True)

    old, new = xa, xb
    for damp, gain in pairs[: S_F - 1]:

        def sweep(r, _, old=old, new=new, damp=damp, gain=gain):
            v = old[r + 1]
            near = old[r] + old[r + 2] + lateral(v, 1, 1)
            resid = rhs[r] - diag[r] * v + near
            d = damp * step[r] + gain * resid
            step[r] = d
            new[r + 1] = v + d
            return 0

        lax.fori_loop(0, NR, sweep, 0, unroll=True)
        old, new = new, old

    even_row = lax.rem(lax.broadcasted_iota(jnp.int32, (ROWS, WIDE), 0), 2) == 0
    even_lane = lax.rem(lanes((HALO, WIDE)), 2) == 0
    pick_r = lax.broadcasted_iota(jnp.int32, (HALO, ROWS), 0)
    pick_c = lax.broadcasted_iota(jnp.int32, (HALO, ROWS), 1)
    pick = jnp.where(lax.shift_right_logical(pick_c, 1) == pick_r, 0.125, 0.0).astype(F32)

    def block_mean(v):
        s = jnp.dot(pick, v, precision=lax.Precision.HIGHEST, preferred_element_type=F32)
        return s + jnp.where(even_lane, pltpu.roll(s, WIDE - 1, 1), pltpu.roll(s, 1, 1))

    def residual(q, _):
        total = None
        diags = None
        for j in range(2):
            r = 2 * q + j
            v = old[r + 1]
            near = old[r] + old[r + 2] + lateral(v, 1, 1)
            resid = (rhs[r] - diag[r] * v + near)[HALO : HALO + ROWS]
            total = resid if total is None else total + resid
            k = diag[r, HALO : HALO + ROWS] - 6.0
            diags = k if diags is None else diags + k
            smooth[r] = v[HALO:, :MAIN]
        packed[q] = jnp.where(even_lane, block_mean(total), block_mean(diags))
        return 0

    lax.fori_loop(0, NR // 2, residual, 0, unroll=True)


def coarse_kernel(ids, near, own, far, smooth, o0, o1, o2, o3, rhs, diag, xa, xb, step, adj):
    first, pairs = coefficients(*COARSE, S_C)
    half = NR // 2
    rows = 3 * HALO
    zero = jnp.zeros((rows, WIDE), F32)
    xa[0] = zero
    xb[0] = zero
    xa[half + 1] = zero
    xb[half + 1] = zero
    even = lax.rem(lanes((HALO, WIDE)), 2) == 0

    def begin(q, _):
        for part, src in (((1 - ids[5]) * 2, near), (1, own), (ids[5] * 2, far)):
            v = src[q]
            at = pl.ds(pl.multiple_of(part * HALO, HALO), HALO)
            rhs[q, at] = jnp.where(even, v, pltpu.roll(v, 1, 1))
            diag[q, at] = jnp.where(even, pltpu.roll(v, WIDE - 1, 1), v) + 1.5
        d = rhs[q] * first
        step[q] = d
        xa[q + 1] = d
        return 0

    lax.fori_loop(0, half, begin, 0, unroll=True)
    old, new = xa, xb
    for damp, gain in pairs[: S_C - 1]:

        def sweep(q, _, old=old, new=new, damp=damp, gain=gain):
            v = old[q + 1]
            around = old[q] + old[q + 2] + lateral(v, 1, 2)
            resid = rhs[q] - diag[q] * v + 0.25 * around
            d = damp * step[q] + gain * resid
            step[q] = d
            new[q + 1] = v + d
            return 0

        lax.fori_loop(0, half, sweep, 0, unroll=True)
        old, new = new, old

    copy_r = lax.broadcasted_iota(jnp.int32, (rows, 2 * HALO), 0)
    copy_c = lax.broadcasted_iota(jnp.int32, (rows, 2 * HALO), 1)
    copy = jnp.where(lax.shift_right_logical(copy_r, 1) == copy_c, 1.0, 0.0).astype(F32)

    def refine(q, _):
        c = jnp.dot(copy, old[q + 1, HALO:, :MAIN], precision=lax.Precision.HIGHEST, preferred_element_type=F32)
        for j in range(2):
            adj[2 * q + j] = smooth[2 * q + j] + c
        return 0

    lax.fori_loop(0, half, refine, 0, unroll=True)
    adj[NR] = jnp.zeros((rows, MAIN), F32)
    for m, out in enumerate((o0, o1, o2, o3)):
        base = (ids[4] ^ m) * LAYERS
        for j in range(LAYERS + 1):
            out[2 * j] = adj[base + j, 0:8]
            out[2 * j + 1] = adj[base + j, 8:16]
        for j in range(LAYERS):
            out[2 * LAYERS + 2, pl.ds(j, 1)] = adj[base + j, 16:17]
        out[2 * LAYERS + 2, pl.ds(LAYERS, 4)] = jnp.zeros((4, MAIN), F32)


def gradient_kernel(ids, p0, p1, p2, p3, forward, forward_x, forward_r, viscosity, adjoint, gradient, above, beyond):
    for m, piece in enumerate((p0, p1, p2, p3)):
        at = pl.ds(pl.multiple_of(ids[m] * MAIN, 128), MAIN)
        for j in range(LAYERS):
            adjoint[j, 0:8, at] = piece[2 * j]
            adjoint[j, 8:16, at] = piece[2 * j + 1]
        above[0:8, at] = piece[2 * LAYERS]
        above[8:16, at] = piece[2 * LAYERS + 1]
        beyond[:, at] = piece[2 * LAYERS + 2]
    last = lax.broadcasted_iota(jnp.int32, (ROWS, 1024), 0) == ROWS - 1
    for j in range(LAYERS):
        a = adjoint[j]
        f = forward[j]
        a_r = (adjoint[j + 1] if j + 1 < LAYERS else above[...]) - a
        f_r = (forward[j + 1] if j + 1 < LAYERS else forward_r[0]) - f
        a_x = jnp.where(last, beyond[pl.ds(j, 1)], pltpu.roll(a, ROWS - 1, 0)) - a
        f_x = jnp.where(last, forward_x[j], pltpu.roll(f, ROWS - 1, 0)) - f
        a_y = pltpu.roll(a, 1023, 1) - a
        f_y = pltpu.roll(f, 1023, 1) - f
        gradient[j] = viscosity[j] * (f_r * a_r + f_x * a_x + f_y * a_y)


def struct(*shape):
    return jax.ShapeDtypeStruct(shape, F32)


def call(kernel, outs, scratch, ids, *args):
    whole = pl.BlockSpec(memory_space=pltpu.VMEM)
    return pl.pallas_call(
        kernel,
        out_shape=outs,
        in_specs=[pl.BlockSpec(memory_space=pltpu.SMEM)] + [whole] * len(args),
        out_specs=[whole] * len(outs),
        scratch_shapes=[pltpu.VMEM(s, F32) for s in scratch],
        compiler_params=VMEM,
    )(ids, *args)


def body(source, kappa, forward, viscosity):
    lat_n = lax.axis_size("lat")
    rad_n = lax.axis_size("rad")
    lat = lax.axis_index("lat")
    rad = lax.axis_index("rad")

    def flip(i):
        return ((i // 4) % 2) * 2

    turn = flip(lat)
    ids = [rad ^ turn, rad ^ 1 ^ turn, rad ^ 2 ^ turn, rad ^ 3 ^ turn, rad, lat % 2]
    ids = jnp.stack(ids).astype(jnp.int32)

    def trade(pieces):
        own, near, far, cross = pieces
        far = lax.ppermute(far, "rad", [(k, k ^ 2) for k in range(rad_n)])
        cross = lax.ppermute(cross, "rad", [(k, k ^ 3) for k in range(rad_n)])
        far, near = lax.optimization_barrier((far, near))
        near = lax.ppermute(near, "rad", [(k, k ^ 1) for k in range(rad_n)])
        return [own, near, far, cross]

    def beside(v, way):
        pairs = []
        for i in range(lat_n):
            to = (i + way) % lat_n
            for k in range(rad_n):
                pairs.append((i * rad_n + k, to * rad_n + (k ^ flip(i) ^ flip(to))))
        return lax.ppermute(v, ("lat", "rad"), pairs)

    def swaps(near, far):
        out = []
        for shift, v in ((1, far), (0, near)):
            pairs = []
            for i in range(lat_n):
                to = (((i + shift) ^ 1) - shift) % lat_n
                for k in range(rad_n):
                    pairs.append((i * rad_n + k, to * rad_n + (k ^ flip(i) ^ flip(to))))
            out.append(lax.ppermute(v, ("lat", "rad"), pairs))
        return out[1], out[0]

    slab = pltpu.VMEM((LAYERS, ROWS, 1024), F32)
    pieces = pl.pallas_call(
        pack_windows,
        out_shape=[struct(LAYERS, ROWS, PACKED)] * 4,
        in_specs=[pl.BlockSpec(memory_space=pltpu.SMEM)] + [pl.BlockSpec(memory_space=pltpu.HBM)] * 2,
        out_specs=[pl.BlockSpec(memory_space=pltpu.VMEM)] * 4,
        scratch_shapes=[slab, slab, pltpu.SemaphoreType.DMA((2, LAYERS))],
        compiler_params=VMEM,
    )(ids, pltpu.with_memory_space_constraint(source, pltpu.HBM), pltpu.with_memory_space_constraint(kappa, pltpu.HBM))
    pieces = trade(pieces)
    first, ahead = lax.optimization_barrier((pieces[2], forward))
    forward_r = lax.ppermute(ahead[:1], "rad", [(k + 1, k) for k in range(rad_n - 1)])
    pieces[2] = first
    up, down = call(pack_rows, [struct(NR, HALO, PACKED)] * 2, [], ids, *pieces)
    up, ahead = lax.optimization_barrier((up, forward))
    lo = beside(up, 1)
    hi = beside(down, -1)
    forward_x = lax.ppermute(ahead[:, :1], "lat", [((i + 1) % lat_n, i) for i in range(lat_n)])
    lo, hi, forward_r = lax.optimization_barrier((lo, hi, forward_r))
    deep = (NR, 2 * ROWS, WIDE)
    padded = (NR + 2, 2 * ROWS, WIDE)
    smooth, packed = call(
        fine_kernel,
        [struct(NR, 3 * HALO, MAIN), struct(NR // 2, HALO, WIDE)],
        [deep, deep, padded, padded, deep],
        ids,
        *pieces,
        lo,
        hi,
    )
    packed, forward_x = lax.optimization_barrier((packed, forward_x))
    near, far = swaps(packed, packed)
    deep = (NR // 2, 3 * HALO, WIDE)
    padded = (NR // 2 + 2, 3 * HALO, WIDE)
    backs = call(
        coarse_kernel,
        [struct(2 * LAYERS + 3, 8, MAIN)] * 4,
        [deep, deep, padded, padded, deep, (NR + 1, 3 * HALO, MAIN)],
        ids,
        near,
        packed,
        far,
        smooth,
    )
    backs = trade(backs)
    adjoint, gradient = call(
        gradient_kernel,
        [struct(LAYERS, ROWS, 1024)] * 2,
        [(ROWS, 1024), (8, 1024)],
        ids,
        *backs,
        forward,
        forward_x,
        forward_r,
        viscosity,
    )
    return adjoint, gradient


def solution(mesh):
    placed = P("rad", "lat", None)
    return jax.shard_map(
        body,
        mesh=mesh,
        in_specs=(placed,) * 4,
        out_specs=(placed,) * 2,
        check_vma=False,
    )
```

```python
import jax
import jax.numpy as jnp
from jax import lax
from jax.experimental import pallas as pl
from jax.experimental.pallas import tpu as pltpu
from jax.sharding import PartitionSpec as P

S_F = 8
S_C = 8
FINE = (1.5, 12.5)
COARSE = (0.05, 3.5)

LAYERS = 4
ROWS = 16
NR = 16
HALO = 8
MAIN = 256
WIDE = 384
PACKED = 640
EDGE = 32
VMEM = pltpu.CompilerParams(vmem_limit_bytes=40 * 1024 * 1024)
F32 = jnp.float32


def lanes(shape):
    return lax.broadcasted_iota(jnp.int32, shape, len(shape) - 1)


def coefficients(low, high, sweeps):
    theta = (high + low) / 2.0
    delta = (high - low) / 2.0
    sigma = theta / delta
    rho = 1.0 / sigma
    pairs = []
    for _ in range(sweeps):
        rho_new = 1.0 / (2.0 * sigma - rho)
        pairs.append((rho_new * rho, 2.0 * rho_new / delta))
        rho = rho_new
    return 1.0 / theta, pairs


def pack_windows(ids, source_hbm, kappa_hbm, *refs):
    outs, (source, kappa, done) = refs[:4], refs[4:]
    loads = []
    for f, (src, dst) in enumerate(((source_hbm, source), (kappa_hbm, kappa))):
        for j in range(LAYERS):
            loads.append(pltpu.make_async_copy(src.at[j], dst.at[j], done.at[f, j]))
            loads[-1].start()
    lane = lanes((ROWS, 128))
    right = lane < EDGE
    left = lane >= 128 - EDGE
    for j in range(LAYERS):
        loads[j].wait()
        loads[LAYERS + j].wait()
        for m, out in enumerate(outs):
            base = ids[m] * MAIN
            main = pl.ds(pl.multiple_of(base, 128), MAIN)
            after = pl.ds(pl.multiple_of(lax.rem(base + MAIN, 1024), 128), 128)
            before = pl.ds(pl.multiple_of(lax.rem(base + 1024 - 128, 1024), 128), 128)
            out[j, :, 0:MAIN] = source[j, :, main]
            out[j, :, MAIN : 2 * MAIN] = kappa[j, :, main]
            edge_s = jnp.where(right, source[j, :, after], source[j, :, before])
            edge_k = jnp.where(right, kappa[j, :, after], kappa[j, :, before])
            edge_k = pltpu.roll(edge_k, 64, 1)
            out[j, :, 2 * MAIN :] = jnp.where(right | left, edge_s, edge_k)


def pack_rows(ids, p0, p1, p2, p3, up, down):
    for m, piece in enumerate((p0, p1, p2, p3)):
        at = pl.ds((ids[4] ^ m) * LAYERS, LAYERS)
        up[at] = piece[:, HALO:, :]
        down[at] = piece[:, :HALO, :]


def spread(packed, rhs, diag):
    lane = lanes(packed.shape[:-1] + (128,))
    keep = (lane < EDGE) | (lane >= 128 - EDGE)
    edge = packed[..., 2 * MAIN :]
    rhs_edge = jnp.where(keep, edge, 0.0)
    diag_edge = jnp.where(keep, pltpu.roll(edge, 64, edge.ndim - 1), 0.0)
    rhs[..., :MAIN] = packed[..., :MAIN]
    rhs[..., MAIN:] = rhs_edge
    diag[..., :MAIN] = packed[..., MAIN : 2 * MAIN] + 6.0
    diag[..., MAIN:] = diag_edge + 6.0


def lateral(v, step_x, step_y):
    rows, width = v.shape
    return (
        pltpu.roll(v, step_x, 0)
        + pltpu.roll(v, rows - step_x, 0)
        + pltpu.roll(v, step_y, 1)
        + pltpu.roll(v, width - step_y, 1)
    )


def fine_kernel(ids, p0, p1, p2, p3, lo, hi, smooth, packed, rhs, diag, xa, xb, step):
    me = ids[4]
    for m, piece in enumerate((p0, p1, p2, p3)):
        base = (me ^ m) * LAYERS

        def fill(j, _, piece=piece, base=base):
            own = pl.ds(HALO, ROWS)
            spread(piece[j], rhs.at[base + j, own], diag.at[base + j, own])
            return 0

        lax.fori_loop(0, LAYERS, fill, 0, unroll=True)

    first, pairs = coefficients(*FINE, S_F)
    zero = jnp.zeros((2 * ROWS, WIDE), F32)
    xa[0] = zero
    xb[0] = zero
    xa[NR + 1] = zero
    xb[NR + 1] = zero

    def begin(r, _):
        spread(lo[r], rhs.at[r, pl.ds(0, HALO)], diag.at[r, pl.ds(0, HALO)])
        top = pl.ds(HALO + ROWS, HALO)
        spread(hi[r], rhs.at[r, top], diag.at[r, top])
        d = rhs[r] * first
        step[r] = d
        xa[r + 1] = d
        return 0

    lax.fori_loop(0, NR, begin, 0, unroll=True)

    old, new = xa, xb
    for damp, gain in pairs[: S_F - 1]:

        def sweep(r, _, old=old, new=new, damp=damp, gain=gain):
            v = old[r + 1]
            near = old[r] + old[r + 2] + lateral(v, 1, 1)
            resid = rhs[r] - diag[r] * v + near
            d = damp * step[r] + gain * resid
            step[r] = d
            new[r + 1] = v + d
            return 0

        lax.fori_loop(0, NR, sweep, 0, unroll=True)
        old, new = new, old

    even_row = lax.rem(lax.broadcasted_iota(jnp.int32, (ROWS, WIDE), 0), 2) == 0
    even_lane = lax.rem(lanes((HALO, WIDE)), 2) == 0
    pick_r = lax.broadcasted_iota(jnp.int32, (HALO, ROWS), 0)
    pick_c = lax.broadcasted_iota(jnp.int32, (HALO, ROWS), 1)
    pick = jnp.where(lax.shift_right_logical(pick_c, 1) == pick_r, 0.125, 0.0).astype(F32)

    def block_mean(v):
        s = jnp.dot(pick, v, precision=lax.Precision.HIGHEST, preferred_element_type=F32)
        return s + jnp.where(even_lane, pltpu.roll(s, WIDE - 1, 1), pltpu.roll(s, 1, 1))

    def residual(q, _):
        total = None
        diags = None
        for j in range(2):
            r = 2 * q + j
            v = old[r + 1]
            near = old[r] + old[r + 2] + lateral(v, 1, 1)
            resid = (rhs[r] - diag[r] * v + near)[HALO : HALO + ROWS]
            total = resid if total is None else total + resid
            k = diag[r, HALO : HALO + ROWS] - 6.0
            diags = k if diags is None else diags + k
            smooth[r] = v[HALO:, :MAIN]
        packed[q] = jnp.where(even_lane, block_mean(total), block_mean(diags))
        return 0

    lax.fori_loop(0, NR // 2, residual, 0, unroll=True)


def coarse_kernel(ids, near, own, far, smooth, o0, o1, o2, o3, rhs, diag, xa, xb, step, adj):
    first, pairs = coefficients(*COARSE, S_C)
    half = NR // 2
    rows = 3 * HALO
    zero = jnp.zeros((rows, WIDE), F32)
    xa[0] = zero
    xb[0] = zero
    xa[half + 1] = zero
    xb[half + 1] = zero
    even = lax.rem(lanes((HALO, WIDE)), 2) == 0

    def begin(q, _):
        for part, src in (((1 - ids[5]) * 2, near), (1, own), (ids[5] * 2, far)):
            v = src[q]
            at = pl.ds(pl.multiple_of(part * HALO, HALO), HALO)
            rhs[q, at] = jnp.where(even, v, pltpu.roll(v, 1, 1))
            diag[q, at] = jnp.where(even, pltpu.roll(v, WIDE - 1, 1), v) + 1.5
        d = rhs[q] * first
        step[q] = d
        xa[q + 1] = d
        return 0

    lax.fori_loop(0, half, begin, 0, unroll=True)
    old, new = xa, xb
    for damp, gain in pairs[: S_C - 1]:

        def sweep(q, _, old=old, new=new, damp=damp, gain=gain):
            v = old[q + 1]
            around = old[q] + old[q + 2] + lateral(v, 1, 2)
            resid = rhs[q] - diag[q] * v + 0.25 * around
            d = damp * step[q] + gain * resid
            step[q] = d
            new[q + 1] = v + d
            return 0

        lax.fori_loop(0, half, sweep, 0, unroll=True)
        old, new = new, old

    copy_r = lax.broadcasted_iota(jnp.int32, (rows, 2 * HALO), 0)
    copy_c = lax.broadcasted_iota(jnp.int32, (rows, 2 * HALO), 1)
    copy = jnp.where(lax.shift_right_logical(copy_r, 1) == copy_c, 1.0, 0.0).astype(F32)

    def refine(q, _):
        c = jnp.dot(copy, old[q + 1, HALO:, :MAIN], precision=lax.Precision.HIGHEST, preferred_element_type=F32)
        for j in range(2):
            adj[2 * q + j] = smooth[2 * q + j] + c
        return 0

    lax.fori_loop(0, half, refine, 0, unroll=True)
    adj[NR] = jnp.zeros((rows, MAIN), F32)
    for m, out in enumerate((o0, o1, o2, o3)):
        base = (ids[4] ^ m) * LAYERS
        for j in range(LAYERS + 1):
            out[2 * j] = adj[base + j, 0:8]
            out[2 * j + 1] = adj[base + j, 8:16]
        for j in range(LAYERS):
            out[2 * LAYERS + 2, pl.ds(j, 1)] = adj[base + j, 16:17]
        out[2 * LAYERS + 2, pl.ds(LAYERS, 4)] = jnp.zeros((4, MAIN), F32)


def gradient_kernel(ids, p0, p1, p2, p3, forward, forward_x, forward_r, viscosity, adjoint, gradient, above, beyond):
    for m, piece in enumerate((p0, p1, p2, p3)):
        at = pl.ds(pl.multiple_of(ids[m] * MAIN, 128), MAIN)
        for j in range(LAYERS):
            adjoint[j, 0:8, at] = piece[2 * j]
            adjoint[j, 8:16, at] = piece[2 * j + 1]
        above[0:8, at] = piece[2 * LAYERS]
        above[8:16, at] = piece[2 * LAYERS + 1]
        beyond[:, at] = piece[2 * LAYERS + 2]
    last = lax.broadcasted_iota(jnp.int32, (ROWS, 1024), 0) == ROWS - 1
    for j in range(LAYERS):
        a = adjoint[j]
        f = forward[j]
        a_r = (adjoint[j + 1] if j + 1 < LAYERS else above[...]) - a
        f_r = (forward[j + 1] if j + 1 < LAYERS else forward_r[0]) - f
        a_x = jnp.where(last, beyond[pl.ds(j, 1)], pltpu.roll(a, ROWS - 1, 0)) - a
        f_x = jnp.where(last, forward_x[j], pltpu.roll(f, ROWS - 1, 0)) - f
        a_y = pltpu.roll(a, 1023, 1) - a
        f_y = pltpu.roll(f, 1023, 1) - f
        gradient[j] = viscosity[j] * (f_r * a_r + f_x * a_x + f_y * a_y)


def struct(*shape):
    return jax.ShapeDtypeStruct(shape, F32)


def call(kernel, outs, scratch, ids, *args):
    whole = pl.BlockSpec(memory_space=pltpu.VMEM)
    return pl.pallas_call(
        kernel,
        out_shape=outs,
        in_specs=[pl.BlockSpec(memory_space=pltpu.SMEM)] + [whole] * len(args),
        out_specs=[whole] * len(outs),
        scratch_shapes=[pltpu.VMEM(s, F32) for s in scratch],
        compiler_params=VMEM,
    )(ids, *args)


def body(source, kappa, forward, viscosity):
    lat_n = lax.axis_size("lat")
    rad_n = lax.axis_size("rad")
    lat = lax.axis_index("lat")
    rad = lax.axis_index("rad")

    def flip(i):
        return ((i // 4) % 2) * 2

    turn = flip(lat)
    ids = [rad ^ turn, rad ^ 1 ^ turn, rad ^ 2 ^ turn, rad ^ 3 ^ turn, rad, lat % 2]
    ids = jnp.stack(ids).astype(jnp.int32)

    def trade(pieces):
        own, near, far, cross = pieces
        far = lax.ppermute(far, "rad", [(k, k ^ 2) for k in range(rad_n)])
        cross = lax.ppermute(cross, "rad", [(k, k ^ 3) for k in range(rad_n)])
        far, near = lax.optimization_barrier((far, near))
        near = lax.ppermute(near, "rad", [(k, k ^ 1) for k in range(rad_n)])
        return [own, near, far, cross]

    def beside(v, way):
        pairs = []
        for i in range(lat_n):
            to = (i + way) % lat_n
            for k in range(rad_n):
                pairs.append((i * rad_n + k, to * rad_n + (k ^ flip(i) ^ flip(to))))
        return lax.ppermute(v, ("lat", "rad"), pairs)

    def swaps(near, far):
        out = []
        for shift, v in ((1, far), (0, near)):
            pairs = []
            for i in range(lat_n):
                to = (((i + shift) ^ 1) - shift) % lat_n
                for k in range(rad_n):
                    pairs.append((i * rad_n + k, to * rad_n + (k ^ flip(i) ^ flip(to))))
            out.append(lax.ppermute(v, ("lat", "rad"), pairs))
        return out[1], out[0]

    slab = pltpu.VMEM((LAYERS, ROWS, 1024), F32)
    pieces = pl.pallas_call(
        pack_windows,
        out_shape=[struct(LAYERS, ROWS, PACKED)] * 4,
        in_specs=[pl.BlockSpec(memory_space=pltpu.SMEM)] + [pl.BlockSpec(memory_space=pltpu.HBM)] * 2,
        out_specs=[pl.BlockSpec(memory_space=pltpu.VMEM)] * 4,
        scratch_shapes=[slab, slab, pltpu.SemaphoreType.DMA((2, LAYERS))],
        compiler_params=VMEM,
    )(ids, pltpu.with_memory_space_constraint(source, pltpu.HBM), pltpu.with_memory_space_constraint(kappa, pltpu.HBM))
    pieces = trade(pieces)
    first, ahead = lax.optimization_barrier((pieces[2], forward))
    forward_r = lax.ppermute(ahead[:1], "rad", [(k + 1, k) for k in range(rad_n - 1)])
    pieces[2] = first
    up, down = call(pack_rows, [struct(NR, HALO, PACKED)] * 2, [], ids, *pieces)
    up, ahead = lax.optimization_barrier((up, forward))
    lo = beside(up, 1)
    hi = beside(down, -1)
    forward_x = lax.ppermute(ahead[:, :1], "lat", [((i + 1) % lat_n, i) for i in range(lat_n)])
    deep = (NR, 2 * ROWS, WIDE)
    padded = (NR + 2, 2 * ROWS, WIDE)
    smooth, packed = call(
        fine_kernel,
        [struct(NR, 3 * HALO, MAIN), struct(NR // 2, HALO, WIDE)],
        [deep, deep, padded, padded, deep],
        ids,
        *pieces,
        lo,
        hi,
    )
    packed, forward_x, forward_r = lax.optimization_barrier((packed, forward_x, forward_r))
    near, far = swaps(packed, packed)
    deep = (NR // 2, 3 * HALO, WIDE)
    padded = (NR // 2 + 2, 3 * HALO, WIDE)
    backs = call(
        coarse_kernel,
        [struct(2 * LAYERS + 3, 8, MAIN)] * 4,
        [deep, deep, padded, padded, deep, (NR + 1, 3 * HALO, MAIN)],
        ids,
        near,
        packed,
        far,
        smooth,
    )
    backs = trade(backs)
    adjoint, gradient = call(
        gradient_kernel,
        [struct(LAYERS, ROWS, 1024)] * 2,
        [(ROWS, 1024), (8, 1024)],
        ids,
        *backs,
        forward,
        forward_x,
        forward_r,
        viscosity,
    )
    return adjoint, gradient


def solution(mesh):
    placed = P("rad", "lat", None)
    return jax.shard_map(
        body,
        mesh=mesh,
        in_specs=(placed,) * 4,
        out_specs=(placed,) * 2,
        check_vma=False,
    )
```

```python
import functools

import jax
import jax.numpy as jnp
from jax import lax
from jax.experimental import pallas as pl
from jax.experimental.pallas import tpu as pltpu
from jax.sharding import PartitionSpec as P

S_F = 8
S_C = 8
FINE = (1.5, 12.5)
COARSE = (0.05, 3.5)

LAYERS = 4
ROWS = 16
NR = 16
HALO = 8
MAIN = 256
WIDE = 384
PACKED = 640
EDGE = 32
VMEM = pltpu.CompilerParams(vmem_limit_bytes=40 * 1024 * 1024)
F32 = jnp.float32


def lanes(shape):
    return lax.broadcasted_iota(jnp.int32, shape, len(shape) - 1)


def coefficients(low, high, sweeps):
    theta = (high + low) / 2.0
    delta = (high - low) / 2.0
    sigma = theta / delta
    rho = 1.0 / sigma
    pairs = []
    for _ in range(sweeps):
        rho_new = 1.0 / (2.0 * sigma - rho)
        pairs.append((rho_new * rho, 2.0 * rho_new / delta))
        rho = rho_new
    return 1.0 / theta, pairs


def pack_windows(members, ids, source_hbm, kappa_hbm, *refs):
    outs, (source, kappa, done) = refs[: len(members)], refs[len(members) :]
    loads = []
    for f, (src, dst) in enumerate(((source_hbm, source), (kappa_hbm, kappa))):
        for j in range(LAYERS):
            loads.append(pltpu.make_async_copy(src.at[j], dst.at[j], done.at[f, j]))
            loads[-1].start()
    lane = lanes((ROWS, 128))
    right = lane < EDGE
    left = lane >= 128 - EDGE
    for j in range(LAYERS):
        loads[j].wait()
        loads[LAYERS + j].wait()
        for m, out in zip(members, outs):
            base = ids[m] * MAIN
            main = pl.ds(pl.multiple_of(base, 128), MAIN)
            after = pl.ds(pl.multiple_of(lax.rem(base + MAIN, 1024), 128), 128)
            before = pl.ds(pl.multiple_of(lax.rem(base + 1024 - 128, 1024), 128), 128)
            out[j, :, 0:MAIN] = source[j, :, main]
            out[j, :, MAIN : 2 * MAIN] = kappa[j, :, main]
            edge_s = jnp.where(right, source[j, :, after], source[j, :, before])
            edge_k = jnp.where(right, kappa[j, :, after], kappa[j, :, before])
            edge_k = pltpu.roll(edge_k, 64, 1)
            out[j, :, 2 * MAIN :] = jnp.where(right | left, edge_s, edge_k)


def pack_rows(ids, p0, p1, p2, p3, up, down):
    for m, piece in enumerate((p0, p1, p2, p3)):
        at = pl.ds((ids[4] ^ m) * LAYERS, LAYERS)
        up[at] = piece[:, HALO:, :]
        down[at] = piece[:, :HALO, :]


def spread(packed, rhs, diag):
    lane = lanes(packed.shape[:-1] + (128,))
    keep = (lane < EDGE) | (lane >= 128 - EDGE)
    edge = packed[..., 2 * MAIN :]
    rhs_edge = jnp.where(keep, edge, 0.0)
    diag_edge = jnp.where(keep, pltpu.roll(edge, 64, edge.ndim - 1), 0.0)
    rhs[..., :MAIN] = packed[..., :MAIN]
    rhs[..., MAIN:] = rhs_edge
    diag[..., :MAIN] = packed[..., MAIN : 2 * MAIN] + 6.0
    diag[..., MAIN:] = diag_edge + 6.0


def lateral(v, step_x, step_y):
    rows, width = v.shape
    return (
        pltpu.roll(v, step_x, 0)
        + pltpu.roll(v, rows - step_x, 0)
        + pltpu.roll(v, step_y, 1)
        + pltpu.roll(v, width - step_y, 1)
    )


def fine_kernel(ids, p0, p1, p2, p3, lo, hi, smooth, packed, rhs, diag, xa, xb, step):
    me = ids[4]
    for m, piece in enumerate((p0, p1, p2, p3)):
        base = (me ^ m) * LAYERS

        def fill(j, _, piece=piece, base=base):
            own = pl.ds(HALO, ROWS)
            spread(piece[j], rhs.at[base + j, own], diag.at[base + j, own])
            return 0

        lax.fori_loop(0, LAYERS, fill, 0, unroll=True)

    first, pairs = coefficients(*FINE, S_F)
    zero = jnp.zeros((2 * ROWS, WIDE), F32)
    xa[0] = zero
    xb[0] = zero
    xa[NR + 1] = zero
    xb[NR + 1] = zero

    def begin(r, _):
        spread(lo[r], rhs.at[r, pl.ds(0, HALO)], diag.at[r, pl.ds(0, HALO)])
        top = pl.ds(HALO + ROWS, HALO)
        spread(hi[r], rhs.at[r, top], diag.at[r, top])
        d = rhs[r] * first
        step[r] = d
        xa[r + 1] = d
        return 0

    lax.fori_loop(0, NR, begin, 0, unroll=True)

    old, new = xa, xb
    for damp, gain in pairs[: S_F - 1]:

        def sweep(r, _, old=old, new=new, damp=damp, gain=gain):
            v = old[r + 1]
            near = old[r] + old[r + 2] + lateral(v, 1, 1)
            resid = rhs[r] - diag[r] * v + near
            d = damp * step[r] + gain * resid
            step[r] = d
            new[r + 1] = v + d
            return 0

        lax.fori_loop(0, NR, sweep, 0, unroll=True)
        old, new = new, old

    even_row = lax.rem(lax.broadcasted_iota(jnp.int32, (ROWS, WIDE), 0), 2) == 0
    even_lane = lax.rem(lanes((HALO, WIDE)), 2) == 0
    pick_r = lax.broadcasted_iota(jnp.int32, (HALO, ROWS), 0)
    pick_c = lax.broadcasted_iota(jnp.int32, (HALO, ROWS), 1)
    pick = jnp.where(lax.shift_right_logical(pick_c, 1) == pick_r, 0.125, 0.0).astype(F32)

    def block_mean(v):
        s = jnp.dot(pick, v, precision=lax.Precision.HIGHEST, preferred_element_type=F32)
        return s + jnp.where(even_lane, pltpu.roll(s, WIDE - 1, 1), pltpu.roll(s, 1, 1))

    def residual(q, _):
        total = None
        diags = None
        for j in range(2):
            r = 2 * q + j
            v = old[r + 1]
            near = old[r] + old[r + 2] + lateral(v, 1, 1)
            resid = (rhs[r] - diag[r] * v + near)[HALO : HALO + ROWS]
            total = resid if total is None else total + resid
            k = diag[r, HALO : HALO + ROWS] - 6.0
            diags = k if diags is None else diags + k
            smooth[r] = v[HALO:, :MAIN]
        packed[q] = jnp.where(even_lane, block_mean(total), block_mean(diags))
        return 0

    lax.fori_loop(0, NR // 2, residual, 0, unroll=True)


def coarse_kernel(ids, near, own, far, smooth, o0, o1, o2, o3, rhs, diag, xa, xb, step, adj):
    first, pairs = coefficients(*COARSE, S_C)
    half = NR // 2
    rows = 3 * HALO
    zero = jnp.zeros((rows, WIDE), F32)
    xa[0] = zero
    xb[0] = zero
    xa[half + 1] = zero
    xb[half + 1] = zero
    even = lax.rem(lanes((HALO, WIDE)), 2) == 0

    def begin(q, _):
        for part, src in (((1 - ids[5]) * 2, near), (1, own), (ids[5] * 2, far)):
            v = src[q]
            at = pl.ds(pl.multiple_of(part * HALO, HALO), HALO)
            rhs[q, at] = jnp.where(even, v, pltpu.roll(v, 1, 1))
            diag[q, at] = jnp.where(even, pltpu.roll(v, WIDE - 1, 1), v) + 1.5
        d = rhs[q] * first
        step[q] = d
        xa[q + 1] = d
        return 0

    lax.fori_loop(0, half, begin, 0, unroll=True)
    old, new = xa, xb
    for damp, gain in pairs[: S_C - 1]:

        def sweep(q, _, old=old, new=new, damp=damp, gain=gain):
            v = old[q + 1]
            around = old[q] + old[q + 2] + lateral(v, 1, 2)
            resid = rhs[q] - diag[q] * v + 0.25 * around
            d = damp * step[q] + gain * resid
            step[q] = d
            new[q + 1] = v + d
            return 0

        lax.fori_loop(0, half, sweep, 0, unroll=True)
        old, new = new, old

    copy_r = lax.broadcasted_iota(jnp.int32, (rows, 2 * HALO), 0)
    copy_c = lax.broadcasted_iota(jnp.int32, (rows, 2 * HALO), 1)
    copy = jnp.where(lax.shift_right_logical(copy_r, 1) == copy_c, 1.0, 0.0).astype(F32)

    def refine(q, _):
        c = jnp.dot(copy, old[q + 1, HALO:, :MAIN], precision=lax.Precision.HIGHEST, preferred_element_type=F32)
        for j in range(2):
            adj[2 * q + j] = smooth[2 * q + j] + c
        return 0

    lax.fori_loop(0, half, refine, 0, unroll=True)
    adj[NR] = jnp.zeros((rows, MAIN), F32)
    for m, out in enumerate((o0, o1, o2, o3)):
        base = (ids[4] ^ m) * LAYERS
        for j in range(LAYERS + 1):
            out[2 * j] = adj[base + j, 0:8]
            out[2 * j + 1] = adj[base + j, 8:16]
        for j in range(LAYERS):
            out[2 * LAYERS + 2, pl.ds(j, 1)] = adj[base + j, 16:17]
        out[2 * LAYERS + 2, pl.ds(LAYERS, 4)] = jnp.zeros((4, MAIN), F32)


def gradient_kernel(ids, p0, p1, p2, p3, forward, forward_x, forward_r, viscosity, adjoint, gradient, above, beyond):
    for m, piece in enumerate((p0, p1, p2, p3)):
        at = pl.ds(pl.multiple_of(ids[m] * MAIN, 128), MAIN)
        for j in range(LAYERS):
            adjoint[j, 0:8, at] = piece[2 * j]
            adjoint[j, 8:16, at] = piece[2 * j + 1]
        above[0:8, at] = piece[2 * LAYERS]
        above[8:16, at] = piece[2 * LAYERS + 1]
        beyond[:, at] = piece[2 * LAYERS + 2]
    last = lax.broadcasted_iota(jnp.int32, (ROWS, 1024), 0) == ROWS - 1
    for j in range(LAYERS):
        a = adjoint[j]
        f = forward[j]
        a_r = (adjoint[j + 1] if j + 1 < LAYERS else above[...]) - a
        f_r = (forward[j + 1] if j + 1 < LAYERS else forward_r[0]) - f
        a_x = jnp.where(last, beyond[pl.ds(j, 1)], pltpu.roll(a, ROWS - 1, 0)) - a
        f_x = jnp.where(last, forward_x[j], pltpu.roll(f, ROWS - 1, 0)) - f
        a_y = pltpu.roll(a, 1023, 1) - a
        f_y = pltpu.roll(f, 1023, 1) - f
        gradient[j] = viscosity[j] * (f_r * a_r + f_x * a_x + f_y * a_y)


def struct(*shape):
    return jax.ShapeDtypeStruct(shape, F32)


def call(kernel, outs, scratch, ids, *args):
    whole = pl.BlockSpec(memory_space=pltpu.VMEM)
    return pl.pallas_call(
        kernel,
        out_shape=outs,
        in_specs=[pl.BlockSpec(memory_space=pltpu.SMEM)] + [whole] * len(args),
        out_specs=[whole] * len(outs),
        scratch_shapes=[pltpu.VMEM(s, F32) for s in scratch],
        compiler_params=VMEM,
    )(ids, *args)


def body(source, kappa, forward, viscosity):
    lat_n = lax.axis_size("lat")
    rad_n = lax.axis_size("rad")
    lat = lax.axis_index("lat")
    rad = lax.axis_index("rad")

    def flip(i):
        return ((i // 4) % 2) * 2

    turn = flip(lat)
    ids = [rad ^ turn, rad ^ 1 ^ turn, rad ^ 2 ^ turn, rad ^ 3 ^ turn, rad, lat % 2]
    ids = jnp.stack(ids).astype(jnp.int32)

    def trade(pieces):
        own, near, far, cross = pieces
        far = lax.ppermute(far, "rad", [(k, k ^ 2) for k in range(rad_n)])
        cross = lax.ppermute(cross, "rad", [(k, k ^ 3) for k in range(rad_n)])
        far, near = lax.optimization_barrier((far, near))
        near = lax.ppermute(near, "rad", [(k, k ^ 1) for k in range(rad_n)])
        return [own, near, far, cross]

    def beside(v, way):
        pairs = []
        for i in range(lat_n):
            to = (i + way) % lat_n
            for k in range(rad_n):
                pairs.append((i * rad_n + k, to * rad_n + (k ^ flip(i) ^ flip(to))))
        return lax.ppermute(v, ("lat", "rad"), pairs)

    def swaps(near, far):
        out = []
        for shift, v in ((1, far), (0, near)):
            pairs = []
            for i in range(lat_n):
                to = (((i + shift) ^ 1) - shift) % lat_n
                for k in range(rad_n):
                    pairs.append((i * rad_n + k, to * rad_n + (k ^ flip(i) ^ flip(to))))
            out.append(lax.ppermute(v, ("lat", "rad"), pairs))
        return out[1], out[0]

    slab = pltpu.VMEM((LAYERS, ROWS, 1024), F32)
    held = [pltpu.with_memory_space_constraint(v, pltpu.HBM) for v in (source, kappa)]

    def windows(*members):
        return pl.pallas_call(
            functools.partial(pack_windows, members),
            out_shape=[struct(LAYERS, ROWS, PACKED)] * len(members),
            in_specs=[pl.BlockSpec(memory_space=pltpu.SMEM)] + [pl.BlockSpec(memory_space=pltpu.HBM)] * 2,
            out_specs=[pl.BlockSpec(memory_space=pltpu.VMEM)] * len(members),
            scratch_shapes=[slab, slab, pltpu.SemaphoreType.DMA((2, LAYERS))],
            compiler_params=VMEM,
        )(ids, *held)

    pieces = [*windows(2, 3)]
    pieces = [*windows(0, 1), *pieces]
    pieces = trade(pieces)
    first, ahead = lax.optimization_barrier((pieces[2], forward))
    forward_r = lax.ppermute(ahead[:1], "rad", [(k + 1, k) for k in range(rad_n - 1)])
    pieces[2] = first
    up, down = call(pack_rows, [struct(NR, HALO, PACKED)] * 2, [], ids, *pieces)
    up, ahead = lax.optimization_barrier((up, forward))
    lo = beside(up, 1)
    hi = beside(down, -1)
    forward_x = lax.ppermute(ahead[:, :1], "lat", [((i + 1) % lat_n, i) for i in range(lat_n)])
    deep = (NR, 2 * ROWS, WIDE)
    padded = (NR + 2, 2 * ROWS, WIDE)
    smooth, packed = call(
        fine_kernel,
        [struct(NR, 3 * HALO, MAIN), struct(NR // 2, HALO, WIDE)],
        [deep, deep, padded, padded, deep],
        ids,
        *pieces,
        lo,
        hi,
    )
    packed, forward_x, forward_r = lax.optimization_barrier((packed, forward_x, forward_r))
    near, far = swaps(packed, packed)
    deep = (NR // 2, 3 * HALO, WIDE)
    padded = (NR // 2 + 2, 3 * HALO, WIDE)
    backs = call(
        coarse_kernel,
        [struct(2 * LAYERS + 3, 8, MAIN)] * 4,
        [deep, deep, padded, padded, deep, (NR + 1, 3 * HALO, MAIN)],
        ids,
        near,
        packed,
        far,
        smooth,
    )
    backs = trade(backs)
    adjoint, gradient = call(
        gradient_kernel,
        [struct(LAYERS, ROWS, 1024)] * 2,
        [(ROWS, 1024), (8, 1024)],
        ids,
        *backs,
        forward,
        forward_x,
        forward_r,
        viscosity,
    )
    return adjoint, gradient


def solution(mesh):
    placed = P("rad", "lat", None)
    return jax.shard_map(
        body,
        mesh=mesh,
        in_specs=(placed,) * 4,
        out_specs=(placed,) * 2,
        check_vma=False,
    )
```
